128 devices in a mesh: ctx: 32 (over z, x, core), head: 4 (over y).
Axes of the slice: x: 4, y: 4, z: 4, core: 2. Of those that a mesh axis runs over, the one named last changes fastest.
Arguments:
- q_raw: bfloat16 [16384, 32, 128], P('ctx', 'head'), may hold values from -12 to 12
- k_raw: bfloat16 [16384, 4, 128], P('ctx', 'head'), may hold values from -12 to 12
- values: bfloat16 [16384, 4, 128], P('ctx', 'head'), may hold values from -6 to 6
- dout: bfloat16 [16384, 32, 128], P('ctx', 'head'), may hold values from -6 to 6
- q_gain: float32 [128], replicated, may hold values from 1 to 6
- k_gain: float32 [128], replicated, may hold values from 1 to 6
- chosen: int32 [32, 4, 8], P('ctx', 'head'), may hold values from -1 to 30, as said below
Outputs:
- dq_raw: bfloat16 [16384, 32, 128], P('ctx', 'head')
- dk_raw: bfloat16 [16384, 4, 128], P('ctx', 'head')
- dvalues: bfloat16 [16384, 4, 128], P('ctx', 'head')
- q_gain_grad: float32 [128], replicated
- k_gain_grad: float32 [128], replicated
The draws below stay inside these ranges and needn't reach their ends.
Inputs may be any that keep to these rules, and one draw needn't show every extreme that they name: chosen[b, g] lists min(8, b) different blocks below b, block b - 1 among them, and -1 in its other slots.
All inputs are finite; a program needn't handle non-finite values.
Results may differ from the reference program's by a relative error of at most 0.02.
The reference program's roundings to bfloat16 on the way (of `qn`, `kn`, `probs_b`, `dscores` and `tile`) count: a program that leaves them out, or rounds other values in their place, can miss the bound.
Values may be sent and summed in bfloat16 or wider, within the bound.
A program may use at most 128 MiB of HBM per device.

```python
import jax
import jax.numpy as jnp
from jax import lax

HD = 128
HEADS = 32
KVH = 4
BLOCK = 512
TOPK = 8
NBLK = 32
TOKENS = 16384


def shared_keys(key):
    return jax.random.normal(jax.random.fold_in(key, 11), (TOKENS, KVH, HD), jnp.float32)


def draw_k_raw(key, part):
    base = shared_keys(key)
    return jnp.clip(base, -12.0, 12.0).astype(jnp.bfloat16)


def draw_q_raw(key, part):
    key = jax.random.fold_in(key, 8)
    queries = jax.random.normal(key, (TOKENS, HEADS, HD), jnp.float32)
    return jnp.clip(queries, -12.0, 12.0).astype(jnp.bfloat16)


def draw_q_gain(key, part):
    key = jax.random.fold_in(key, 3)
    return jax.random.uniform(key, (HD,), jnp.float32, 1.0, 2.2)


def draw_k_gain(key, part):
    key = jax.random.fold_in(key, 4)
    return jax.random.uniform(key, (HD,), jnp.float32, 1.0, 2.2)


def draw_chosen(key, part):
    key = jax.random.fold_in(key, 5)
    noise = jax.random.randint(key, (NBLK, KVH, NBLK), 0, 4096)
    col = jnp.arange(NBLK, dtype=jnp.int32)[None, None, :]
    row = jnp.arange(NBLK, dtype=jnp.int32)[:, None, None]
    early = (NBLK - 1 - col) * 8192 // max(NBLK - 1, 1)
    prior = noise + early + jnp.where(col == row - 1, 1 << 20, 0)
    prior = prior * NBLK + col
    prior = jnp.where(col < row, prior, -1 - col)
    top_vals, top_ids = lax.top_k(prior, TOPK)
    return jnp.where(top_vals >= 0, top_ids, -1).astype(jnp.int32)


def block_levels(key, extent, pieces, low, top_value):
    def one(axis_at, shards_of):
        draws = jax.random.uniform(jax.random.fold_in(jax.random.fold_in(key, 6), axis_at), (shards_of,), jnp.float32, low / len(pieces), top_value / len(pieces))
        return jnp.repeat(jnp.exp(draws), extent[axis_at] // shards_of).reshape((-1,) + (1,) * (len(extent) - axis_at - 1))

    level = one(*pieces[0])
    for cut in pieces[1:]:
        level = level * one(*cut)
    return level


def normal_values(own_key, shape, deviation, reach, pieces=(), kind=jnp.bfloat16):
    entries = deviation * jax.random.normal(own_key, shape, jnp.float32)
    if pieces:
        entries = entries * block_levels(own_key, shape, pieces, -0.22, 0.18)
    return jnp.clip(entries, -reach, reach).astype(kind)


def setup_inputs(seed: int = 0) -> dict:
    seeds = jax.random.split(jax.random.key(seed), 8)
    q_raw = draw_q_raw(jax.random.fold_in(seeds[7], 71), 0)
    k_raw = draw_k_raw(jax.random.fold_in(seeds[7], 71), 0)
    values = normal_values(seeds[2], (TOKENS, KVH, HD), 1.0, 6.0, ((0, 32), (1, 4)))
    dout = normal_values(seeds[3], (TOKENS, HEADS, HD), 1.0, 6.0, ((0, 32), (1, 4)))
    q_gain = draw_q_gain(jax.random.fold_in(seeds[7], 71), 0)
    k_gain = draw_k_gain(jax.random.fold_in(seeds[7], 71), 0)
    chosen = draw_chosen(jax.random.fold_in(seeds[7], 71), 0)
    return {"q_raw": q_raw, "k_raw": k_raw, "values": values, "dout": dout, "q_gain": q_gain, "k_gain": k_gain, "chosen": chosen}


EPS = 1e-06

def norm_fwd(raw, gain):
    x = raw.astype(jnp.float32)
    scale_r = lax.rsqrt(lax.optimization_barrier(jnp.mean(x * x, axis=-1, keepdims=True)) + EPS)
    return (x, scale_r, (x * scale_r * gain).astype(jnp.bfloat16))

def norm_back(x, scale_r, gain, grad_y):
    along = gain * grad_y
    inner = lax.optimization_barrier(jnp.mean(along * x, axis=-1, keepdims=True))
    grad_x = scale_r * (along - x * scale_r * scale_r * inner)
    return (grad_x, grad_y * x * scale_r)

def block_grads(q_grp, do_grp, keys, vals, valid):
    blk = q_grp.shape[1]
    slots = keys.shape[0] // blk
    scale = 1.0 / jnp.sqrt(jnp.float32(keys.shape[1]))
    rows = lax.broadcasted_iota(jnp.int32, (blk, blk), 0)
    cols = lax.broadcasted_iota(jnp.int32, (blk, blk), 1)
    chosen_mask = jnp.broadcast_to(jnp.repeat(valid, blk)[None, :], (blk, (slots - 1) * blk))
    mask = jnp.concatenate([chosen_mask, cols <= rows], axis=1)

    def one_head(carry, inputs):
        qh, doh = inputs
        scores = jnp.dot(qh, keys.T, preferred_element_type=jnp.float32) * scale
        scores = jnp.where(mask, scores, -jnp.inf)
        top = lax.optimization_barrier(jnp.max(scores, axis=1, keepdims=True))
        expo = jnp.exp(scores - top)
        probs = expo / lax.optimization_barrier(jnp.sum(expo, axis=1, keepdims=True))
        probs_b = probs.astype(jnp.bfloat16)
        attn_out = jnp.dot(probs_b, vals, preferred_element_type=jnp.float32)
        delta = lax.optimization_barrier(jnp.sum(doh.astype(jnp.float32) * attn_out, axis=1, keepdims=True))
        dprobs = jnp.dot(doh, vals.T, preferred_element_type=jnp.float32)
        dscores = (probs * (dprobs - delta)).astype(jnp.bfloat16)
        dq = jnp.dot(dscores, keys, preferred_element_type=jnp.float32) * scale
        dk = carry[0] + jnp.dot(dscores.T, qh, preferred_element_type=jnp.float32) * scale
        dv = carry[1] + jnp.dot(probs_b.T, doh, preferred_element_type=jnp.float32)
        return ((dk, dv), dq)
    zeros = jnp.zeros(keys.shape, jnp.float32)
    (dk, dv), dq = lax.scan(one_head, (zeros, zeros), (q_grp, do_grp))
    return (dq, dk, dv)

def reference(q_raw, k_raw, values, dout, q_gain, k_gain, chosen):
    xq, rq, qn = norm_fwd(q_raw, q_gain)
    xk, rk, kn = norm_fwd(k_raw, k_gain)
    group = HEADS // KVH
    knb = kn.reshape(NBLK, BLOCK, KVH, HD)
    vb = values.reshape(NBLK, BLOCK, KVH, HD)
    qnb = qn.reshape(NBLK, BLOCK, HEADS, HD)
    dob = dout.reshape(NBLK, BLOCK, HEADS, HD)

    def per_block(acc, blk):
        qblk = lax.dynamic_index_in_dim(qnb, blk, 0, keepdims=False)
        doblk = lax.dynamic_index_in_dim(dob, blk, 0, keepdims=False)
        idx_row = lax.dynamic_index_in_dim(chosen, blk, 0, keepdims=False)
        dq_parts = []
        for gidx in range(KVH):
            idx = idx_row[gidx]
            valid = idx >= 0
            idxc = jnp.maximum(idx, 0).astype(jnp.int32)
            own = jnp.reshape(blk, (1,)).astype(jnp.int32)
            full_idx = jnp.concatenate([idxc, own])
            keys = knb[full_idx, :, gidx].reshape(-1, HD)
            vals = vb[full_idx, :, gidx].reshape(-1, HD)
            q_grp = jnp.transpose(qblk[:, gidx * group:(gidx + 1) * group], (1, 0, 2))
            do_grp = jnp.transpose(doblk[:, gidx * group:(gidx + 1) * group], (1, 0, 2))
            dq, dk, dv = block_grads(q_grp, do_grp, keys, vals, valid)
            dq_parts.append(jnp.transpose(dq, (1, 0, 2)))
            tile = jnp.concatenate([dk, dv], axis=1).reshape(TOPK + 1, BLOCK, 2 * HD)
            tile = lax.optimization_barrier(tile.astype(jnp.bfloat16)).astype(jnp.float32)
            weight = jnp.concatenate([valid, jnp.ones((1,), bool)]).astype(jnp.float32)
            tile = tile * weight[:, None, None]
            acc = acc.at[full_idx, :, gidx, :].add(tile)
        return (acc, jnp.concatenate(dq_parts, axis=1))
    acc0 = jnp.zeros((NBLK, BLOCK, KVH, 2 * HD), jnp.float32)
    dkv, dqn = lax.scan(per_block, acc0, jnp.arange(NBLK, dtype=jnp.int32))
    dkv = dkv.reshape(TOKENS, KVH, 2 * HD)
    dqn = dqn.reshape(TOKENS, HEADS, HD)
    dkn = dkv[..., :HD]
    dvalues = dkv[..., HD:].astype(jnp.bfloat16)
    dq_raw, gq = norm_back(xq, rq, q_gain, dqn)
    dk_raw, gk = norm_back(xk, rk, k_gain, dkn)
    q_gain_grad = lax.optimization_barrier(jnp.sum(gq.reshape(-1, HD), axis=0))
    k_gain_grad = lax.optimization_barrier(jnp.sum(gk.reshape(-1, HD), axis=0))
    return (dq_raw.astype(jnp.bfloat16), dk_raw.astype(jnp.bfloat16), dvalues, q_gain_grad, k_gain_grad)
```

```python
import functools

import jax, jax.numpy as jnp
from jax import lax
from jax.experimental import pallas as pl
from jax.experimental.pallas import tpu as pltpu
from jax.sharding import PartitionSpec as P

SC = 128 ** -0.5
C2 = SC * 1.4426950408889634
NEG = -1e30
F32 = jnp.float32
BF = jnp.bfloat16

EPS = 1e-06


def norm_fwd(raw, gain):
    x = raw.astype(jnp.float32)
    scale_r = lax.rsqrt(jnp.mean(x * x, axis=-1, keepdims=True) + EPS)
    return (x, scale_r, (x * scale_r * gain).astype(jnp.bfloat16))


def norm_back(x, scale_r, gain, grad_y):
    along = gain * grad_y
    inner = jnp.mean(along * x, axis=-1, keepdims=True)
    grad_x = scale_r * (along - x * scale_r * scale_r * inner)
    return (grad_x, grad_y * x * scale_r)


def dot(a, b):
    return lax.dot_general(a, b, (((1,), (0,)), ((), ())), preferred_element_type=F32)

def fold(x, op):
    return op(x.reshape(x.shape[0] // 8, 8, x.shape[1]), axis=0)

def attn_kernel(idx_ref, kv_hbm, q_ref, qT_ref, do_ref, doT_ref,
                dq_ref, tile_ref, kg_ref,
                kb, vb, kT, vT, S, E, dk, dv, oT, dqT, mrow, drow, qs, dos, sem):
    H = q_ref.shape[0]
    J = 9
    me = lax.axis_index("ctx")
    cps = []
    for j in range(J):
        blk = jnp.maximum(idx_ref[j], 0) if j < 8 else me
        cps.append((pltpu.make_async_copy(kv_hbm.at[blk, :, 0:128], kb.at[j], sem.at[0, j]),
                    pltpu.make_async_copy(kv_hbm.at[blk, :, 128:256], vb.at[j], sem.at[1, j])))
    for a, b in cps:
        a.start(); b.start()
    for a, b in cps:
        a.wait(); b.wait()

    @pl.loop(0, J)
    def _(j):
        kT[j] = kb[j].T
        vT[j] = vb[j].T
        dk[j] = jnp.zeros(dk.shape[1:], F32)
        dv[j] = jnp.zeros(dv.shape[1:], F32)

    rows = lax.broadcasted_iota(jnp.int32, (512, 512), 0)
    cols = lax.broadcasted_iota(jnp.int32, (512, 512), 1)

    def A1(h, j, own):
        s = dot(kb[j], qT_ref[h])
        if own:
            s = jnp.where(rows <= cols, s, NEG)
        S[h % 2, j] = s
        cm = fold(s, jnp.max)
        if not own:
            cm = jnp.where(idx_ref[j] >= 0, cm, NEG)
        return cm

    def A2(h, j, own):
        m = mrow[h % 2]
        if not own:
            m = jnp.where(idx_ref[j] >= 0, m, 1e30)
        s = S[h % 2, j]
        e = jnp.exp2((s.reshape(64, 8, 512) - m[None]) * C2)
        l = jnp.sum(e, axis=0)
        eb = e.reshape(512, 512).astype(BF)
        E[h % 2, j] = eb
        oT[...] += dot(vT[j], eb)
        return l

    def C(h, j):
        dp = dot(vb[j], doT_ref[h])
        dl = drow[h % 2]
        dpb = (dp.reshape(64, 8, 512) - dl[None]).reshape(512, 512).astype(BF)
        eb = E[h % 2, j]
        ds = eb * dpb
        dv[j] += dot(eb, dos[h % 2])
        dk[j] += dot(ds, qs[h % 2])
        dqT[...] += dot(kT[j], ds)

    def step(t, a1, a2, c):
        if a2:
            oT[...] = jnp.zeros(oT.shape, F32)
        if c:
            dqT[...] = jnp.zeros(dqT.shape, F32)

        def body(j, carry, own=False):
            mx, l = carry
            if a1:
                mx = jnp.maximum(mx, A1(t, j, own))
            if a2:
                l = l + A2(t - 1, j, own)
            if c:
                C(t - 2, j)
            return mx, l
        carry = (jnp.full((8, 512), NEG, F32), jnp.zeros((8, 512), F32))
        carry = lax.fori_loop(0, J - 1, body, carry)
        mx, l = body(J - 1, carry, True)
        if c:
            h = t - 2
            rl = drow[h % 2 + 2]
            dq_ref[h] = (dqT[...] * (rl[:1] * SC)).T
        if a2:
            h = t - 1
            l1 = jnp.sum(l, axis=0, keepdims=True)
            rl = jnp.broadcast_to(1.0 / l1, (8, 512))
            o = oT[...]
            dl = jnp.sum(o * doT_ref[h].astype(F32), axis=0, keepdims=True) * rl[:1]
            drow[h % 2] = jnp.broadcast_to(dl, (8, 512))
            drow[h % 2 + 2] = rl
            rc = rl.T[:, :1]
            dos[h % 2] = (do_ref[h].astype(F32) * rc).astype(BF)
            qs[h % 2] = (q_ref[h].astype(F32) * (rc * SC)).astype(BF)
        if a1:
            m = jnp.max(mx, axis=0, keepdims=True)
            mrow[t % 2] = jnp.broadcast_to(m, (8, 512))

    step(0, True, False, False)
    step(1, True, True, False)

    @pl.loop(2, H)
    def _(t):
        step(t, True, True, True)
    step(H, False, True, True)
    step(H + 1, False, False, True)

    kg_ref[...] = jnp.zeros(kg_ref.shape, F32)

    @pl.loop(0, J)
    def _(j):
        kg_ref[...] += fold(dk[j] * kb[j].astype(F32), jnp.sum)
        tile_ref[j, :, 0:128] = dk[j].astype(BF)
        tile_ref[j, :, 128:256] = dv[j].astype(BF)


def attn(idx, kv_all, q, qT, do, doT):
    H = q.shape[0]
    V = functools.partial(pl.BlockSpec, memory_space=pltpu.VMEM)
    return pl.pallas_call(
        attn_kernel,
        out_shape=(
            jax.ShapeDtypeStruct((H, 512, 128), F32),
            jax.ShapeDtypeStruct((9, 512, 256), BF),
            jax.ShapeDtypeStruct((8, 128), F32),
        ),
        in_specs=[pl.BlockSpec(memory_space=pltpu.SMEM), pl.BlockSpec(memory_space=pl.ANY), V(), V(), V(), V()],
        out_specs=(V(), V(), V()),
        scratch_shapes=[
            pltpu.VMEM((9, 512, 128), BF), pltpu.VMEM((9, 512, 128), BF),
            pltpu.VMEM((9, 128, 512), BF), pltpu.VMEM((9, 128, 512), BF),
            pltpu.VMEM((2, 9, 512, 512), F32), pltpu.VMEM((2, 9, 512, 512), BF),
            pltpu.VMEM((9, 512, 128), F32), pltpu.VMEM((9, 512, 128), F32),
            pltpu.VMEM((128, 512), F32), pltpu.VMEM((128, 512), F32),
            pltpu.VMEM((2, 8, 512), F32), pltpu.VMEM((4, 8, 512), F32),
            pltpu.VMEM((2, 512, 128), BF), pltpu.VMEM((2, 512, 128), BF),
            pltpu.SemaphoreType.DMA((2, 9)),
        ],
        compiler_params=pltpu.CompilerParams(vmem_limit_bytes=60 * 2 ** 20),
    )(idx, kv_all, q, qT, do, doT)


def on_device(q_raw, k_raw, values, dout, q_gain, k_gain, chosen):
    blk, heads, width = q_raw.shape
    position = lax.axis_index("ctx")
    k2, v2 = k_raw.reshape(blk, width), values.reshape(blk, width)
    xk, rk, kn = norm_fwd(k2, k_gain)
    kv_all = lax.all_gather(jnp.concatenate([kn, v2], axis=1), "ctx", axis=0)
    xq, rq, qn = norm_fwd(jnp.transpose(q_raw, (1, 0, 2)), q_gain)
    do = jnp.transpose(dout, (1, 0, 2))
    idx = chosen.reshape(-1)
    dq, tile, kg = attn(idx, kv_all, qn, jnp.swapaxes(qn, 1, 2), do, jnp.swapaxes(do, 1, 2))
    dq_raw, gq = norm_back(xq, rq, q_gain, dq)
    part_q = jnp.sum(gq.reshape(-1, width), axis=0)
    part_k = jnp.sum(kg, axis=0) / k_gain
    q_gain_grad, k_gain_grad = lax.psum((part_q, part_k), ("ctx", "head"))
    target = jnp.concatenate([idx, position[None]])
    onehot = target[None, :] == jnp.arange(32, dtype=jnp.int32)[:, None]
    slot = jnp.argmax(onehot, axis=1)
    hit = jnp.any(onehot, axis=1)
    term = jnp.where(hit[:, None, None], tile[slot], 0).reshape(32 * blk, 2 * width)
    dkv = lax.psum_scatter(term, "ctx", scatter_dimension=0, tiled=True).astype(F32)
    dk_raw, _ = norm_back(xk, rk, k_gain, dkv[:, :width])
    return (
        jnp.transpose(dq_raw.astype(BF), (1, 0, 2)),
        dk_raw.astype(BF).reshape(blk, 1, width),
        dkv[:, width:].astype(BF).reshape(blk, 1, width),
        q_gain_grad,
        k_gain_grad,
    )


def solution(mesh):
    tok = P("ctx", "head", None)
    return jax.shard_map(
        on_device,
        mesh=mesh,
        in_specs=(tok, tok, tok, tok, P(), P(), tok),
        out_specs=(tok, tok, tok, P(), P()),
        check_vma=False,
    )
```

```python
import functools

import jax, jax.numpy as jnp
from jax import lax
from jax.experimental import pallas as pl
from jax.experimental.pallas import tpu as pltpu
from jax.sharding import PartitionSpec as P

SC = 128 ** -0.5
C2 = SC * 1.4426950408889634
NEG = -1e30
F32 = jnp.float32
BF = jnp.bfloat16

EPS = 1e-06


def norm_fwd(raw, gain):
    x = raw.astype(jnp.float32)
    scale_r = lax.rsqrt(jnp.mean(x * x, axis=-1, keepdims=True) + EPS)
    return (x, scale_r, (x * scale_r * gain).astype(jnp.bfloat16))


def norm_back(x, scale_r, gain, grad_y):
    along = gain * grad_y
    inner = jnp.mean(along * x, axis=-1, keepdims=True)
    grad_x = scale_r * (along - x * scale_r * scale_r * inner)
    return (grad_x, grad_y * x * scale_r)


def dot(a, b):
    return lax.dot_general(a, b, (((1,), (0,)), ((), ())), preferred_element_type=F32)

def fold(x, op):
    return op(x.reshape(x.shape[0] // 8, 8, x.shape[1]), axis=0)

def attn_kernel(idx_ref, kv_hbm, q_ref, qT_ref, do_ref, doT_ref,
                dq_ref, tile_ref, kg_ref,
                kb, vb, kT, vT, S, E, dk, dv, oT, dqT, mrow, drow, qs, dos, sem):
    H = q_ref.shape[0]
    J = 9
    me = lax.axis_index("ctx")
    cps = []
    for j in range(J):
        blk = jnp.maximum(idx_ref[j], 0) if j < 8 else me
        cps.append((pltpu.make_async_copy(kv_hbm.at[blk, :, 0:128], kb.at[j], sem.at[0, j]),
                    pltpu.make_async_copy(kv_hbm.at[blk, :, 128:256], vb.at[j], sem.at[1, j])))
    for a, b in cps:
        a.start(); b.start()
    for a, b in cps:
        a.wait(); b.wait()

    @pl.loop(0, J)
    def _(j):
        kT[j] = kb[j].T
        vT[j] = vb[j].T
        dk[j] = jnp.zeros(dk.shape[1:], F32)
        dv[j] = jnp.zeros(dv.shape[1:], F32)

    rows = lax.broadcasted_iota(jnp.int32, (512, 512), 0)
    cols = lax.broadcasted_iota(jnp.int32, (512, 512), 1)

    def A1(h, j, own):
        s = dot(kb[j], qT_ref[h])
        if own:
            s = jnp.where(rows <= cols, s, NEG)
        S[h % 2, j] = s
        cm = fold(s, jnp.max)
        if not own:
            cm = jnp.where(idx_ref[j] >= 0, cm, NEG)
        return cm

    def A2(h, j, own):
        m = mrow[h % 2]
        if not own:
            m = jnp.where(idx_ref[j] >= 0, m, 1e30)
        s = S[h % 2, j]
        e = jnp.exp2((s.reshape(64, 8, 512) - m[None]) * C2)
        l = jnp.sum(e, axis=0)
        eb = e.reshape(512, 512).astype(BF)
        E[h % 2, j] = eb
        oT[...] += dot(vT[j], eb)
        return l

    def C(h, j):
        dp = dot(vb[j], doT_ref[h])
        dl = drow[h % 2]
        dpb = (dp.reshape(64, 8, 512) - dl[None]).reshape(512, 512).astype(BF)
        eb = E[h % 2, j]
        ds = eb * dpb
        dv[j] += dot(eb, dos[h % 2])
        dk[j] += dot(ds, qs[h % 2])
        dqT[...] += dot(kT[j], ds)

    def step(t, a1, a2, c):
        if a2:
            oT[...] = jnp.zeros(oT.shape, F32)
        if c:
            dqT[...] = jnp.zeros(dqT.shape, F32)

        def body(j, carry, own=False):
            mx, l = carry
            if a1:
                mx = jnp.maximum(mx, A1(t, j, own))
            if a2:
                l = l + A2(t - 1, j, own)
            if c:
                C(t - 2, j)
            return mx, l
        carry = (jnp.full((8, 512), NEG, F32), jnp.zeros((8, 512), F32))
        carry = lax.fori_loop(0, J - 1, body, carry)
        mx, l = body(J - 1, carry, True)
        if c:
            h = t - 2
            rl = drow[h % 2 + 2]
            dq_ref[h] = (dqT[...] * (rl[:1] * SC)).T
        if a2:
            h = t - 1
            l1 = jnp.sum(l, axis=0, keepdims=True)
            rl = jnp.broadcast_to(1.0 / l1, (8, 512))
            o = oT[...]
            dl = jnp.sum(o * doT_ref[h].astype(F32), axis=0, keepdims=True) * rl[:1]
            drow[h % 2] = jnp.broadcast_to(dl, (8, 512))
            drow[h % 2 + 2] = rl
            rc = rl.T[:, :1]
            dos[h % 2] = (do_ref[h].astype(F32) * rc).astype(BF)
            qs[h % 2] = (q_ref[h].astype(F32) * (rc * SC)).astype(BF)
        if a1:
            m = jnp.max(mx, axis=0, keepdims=True)
            mrow[t % 2] = jnp.broadcast_to(m, (8, 512))

    step(0, True, False, False)
    step(1, True, True, False)

    @pl.loop(2, H)
    def _(t):
        step(t, True, True, True)
    step(H, False, True, True)
    step(H + 1, False, False, True)

    kg_ref[...] = jnp.zeros(kg_ref.shape, F32)
    tile_ref[J] = jnp.zeros(tile_ref.shape[1:], BF)

    @pl.loop(0, J)
    def _(j):
        kg_ref[...] += fold(dk[j] * kb[j].astype(F32), jnp.sum)
        tile_ref[j, :, 0:128] = dk[j].astype(BF)
        tile_ref[j, :, 128:256] = dv[j].astype(BF)


MESH = pl.DeviceIdType.MESH


def place():
    ctx, y = lax.axis_index("ctx"), lax.axis_index("head")
    return ctx // 8, (ctx // 2) % 4, ctx % 2, y


def peer(z, x, c, y):
    return (z * 8 + x * 2 + c, y)


def greet(devices):
    barrier = pltpu.get_barrier_semaphore()
    for d in devices:
        pl.semaphore_signal(barrier, inc=1, device_id=d, device_id_type=MESH)
    pl.semaphore_wait(barrier, len(devices))


def scatter_kernel(slot_ref, tile_ref, g_ref, dk_ref, dv_ref, gout_ref,
                   A, B, cur, R1, R2, T, Q1, Q2, GS, GZ, GX, GY,
                   s0, r0, s1, r1, s2, r2, sg, rg):
    z, x, c, y = place()

    def along(axis, off):
        if axis == "z":
            return peer((z + off) % 4, x, c, y)
        if axis == "x":
            return peer(z, (x + off) % 4, c, y)
        return peer(z, x, c, (y + off) % 4)

    sib = peer(z, x, 1 - c, y)
    greet([sib] + [along(a, o) for a in "zxy" for o in (1, 2, 3)])
    pending = []

    def send(src, dst, ss, rs, to):
        cp = pltpu.make_async_remote_copy(src_ref=src, dst_ref=dst, send_sem=ss, recv_sem=rs,
                                          device_id=to, device_id_type=MESH)
        cp.start()
        pending.append(cp)
        return cp

    gcp = send(g_ref, GS, sg.at[0], rg.at[0], sib)

    axes = (("z", "x"), ("x", "z"))
    coord = {"z": z, "x": x}

    def block(half, u, w, cc):
        return (u * 8 + w * 2 + cc) if half == 0 else (w * 8 + u * 2 + cc)

    def cols(half):
        return slice(half * 128, half * 128 + 128)

    first = {}
    for off in (2, 1, 3, 0):
        for half in (0, 1):
            u = (coord[axes[half][0]] + off) % 4

            @pl.loop(0, 4)
            def _(w):
                A[half, off, w] = tile_ref[slot_ref[block(half, u, w, 1 - c)], :, cols(half)]
            first[half, off] = send(A.at[half, off], B.at[half, off], s0.at[half * 4 + off], r0.at[half * 4 + off], sib)

    def group(G, base, kind):
        me = {"z": z, "x": x, "y": y}[kind]
        cps = [send(G.at[me], G.at[me], sg.at[base + o], rg.at[base + o], along(kind, o)) for o in (1, 2, 3)]
        return cps

    def gsum(G, cps):
        for cp in cps:
            cp.wait_recv()
        return (G[0] + G[1]) + (G[2] + G[3])

    def own_sum(half, off):
        first[half, off].wait_recv()
        u = (coord[axes[half][0]] + off) % 4

        @pl.loop(0, 4)
        def _(w):
            mine = tile_ref[slot_ref[block(half, u, w, c)], :, cols(half)]
            cur[half, off, w] = (mine.astype(F32) + B[half, off, w].astype(F32)).astype(BF)

    def s1send(k, half, src, dst, off):
        return send(src, dst, s1.at[half, k], r1.at[half, k], along(axes[half][0], off))

    c1 = {}
    for half in (0, 1):
        own_sum(half, 2)
        c1[half, 0] = s1send(0, half, cur.at[half, 2, 0:2], R1.at[half, 0], 1)
        c1[half, 1] = s1send(1, half, cur.at[half, 2, 2:4], R1.at[half, 1], 3)
    for half in (0, 1):
        own_sum(half, 1)
        c1[half, 2] = s1send(2, half, cur.at[half, 1, 2:4], R2.at[half, 0, 2:4], 1)
        own_sum(half, 3)
        c1[half, 3] = s1send(3, half, cur.at[half, 3, 0:2], R2.at[half, 1, 0:2], 3)
    gcp.wait_recv()
    GZ[z] = g_ref[...] + GS[...]
    gz = group(GZ, 0, "z")
    for half in (0, 1):
        own_sum(half, 0)
    for half in (0, 1):
        c1[half, 0].wait_recv()

        @pl.loop(0, 2)
        def _(w):
            cur[half, 1, w] = (cur[half, 1, w].astype(F32) + R1[half, 0, w].astype(F32)).astype(BF)
        c1[half, 4] = s1send(4, half, cur.at[half, 1, 0:2], R2.at[half, 0, 0:2], 1)
        c1[half, 1].wait_recv()

        @pl.loop(0, 2)
        def _(w):
            cur[half, 3, w + 2] = (cur[half, 3, w + 2].astype(F32) + R1[half, 1, w].astype(F32)).astype(BF)
        c1[half, 5] = s1send(5, half, cur.at[half, 3, 2:4], R2.at[half, 1, 2:4], 3)
    GX[x] = gsum(GZ, gz)
    gx = group(GX, 3, "x")

    def s2send(k, half, src, dst, off):
        return send(src, dst, s2.at[half, k], r2.at[half, k], along(axes[half][1], off))

    lo, hi = slice(0, 256), slice(256, 512)
    c2 = {}
    for half in (0, 1):
        for k in (2, 3, 4, 5):
            c1[half, k].wait_recv()
        cw = coord[axes[half][1]]

        @pl.loop(0, 4)
        def _(o):
            w = (cw + o) % 4
            T[half, o] = (cur[half, 0, w].astype(F32) + R2[half, 0, w].astype(F32)
                          + R2[half, 1, w].astype(F32)).astype(BF)
        c2[half, 0] = s2send(0, half, T.at[half, 2, lo], Q1.at[half, 0], 1)
        c2[half, 1] = s2send(1, half, T.at[half, 2, hi], Q1.at[half, 1], 3)
        c2[half, 2] = s2send(2, half, T.at[half, 1, hi], Q2.at[half, 0, hi], 1)
        c2[half, 3] = s2send(3, half, T.at[half, 3, lo], Q2.at[half, 1, lo], 3)
    GY[y] = gsum(GX, gx)
    gy = group(GY, 6, "y")
    for half in (0, 1):
        c2[half, 0].wait_recv()
        T[half, 1, lo] = (T[half, 1, lo].astype(F32) + Q1[half, 0].astype(F32)).astype(BF)
        c2[half, 4] = s2send(4, half, T.at[half, 1, lo], Q2.at[half, 0, lo], 1)
        c2[half, 1].wait_recv()
        T[half, 3, hi] = (T[half, 3, hi].astype(F32) + Q1[half, 1].astype(F32)).astype(BF)
        c2[half, 5] = s2send(5, half, T.at[half, 3, hi], Q2.at[half, 1, hi], 3)
    gout_ref[...] = gsum(GY, gy)
    for half in (0, 1):
        for k in (2, 3, 4, 5):
            c2[half, k].wait_recv()
        out = T[half, 0].astype(F32) + Q2[half, 0].astype(F32) + Q2[half, 1].astype(F32)
        if half == 0:
            dk_ref[...] = out
        else:
            dv_ref[...] = out.astype(BF)
    for cp in pending:
        cp.wait_send()


def scatter(slot, tile, g):
    V = functools.partial(pl.BlockSpec, memory_space=pltpu.VMEM)
    D = pltpu.SemaphoreType.DMA
    return pl.pallas_call(
        scatter_kernel,
        out_shape=(jax.ShapeDtypeStruct((512, 128), F32), jax.ShapeDtypeStruct((512, 128), BF),
                   jax.ShapeDtypeStruct((8, 128), F32)),
        in_specs=[pl.BlockSpec(memory_space=pltpu.SMEM), V(), V()],
        out_specs=(V(), V(), V()),
        scratch_shapes=[
            pltpu.VMEM((2, 4, 4, 512, 128), BF), pltpu.VMEM((2, 4, 4, 512, 128), BF), pltpu.VMEM((2, 4, 4, 512, 128), BF),
            pltpu.VMEM((2, 2, 2, 512, 128), BF), pltpu.VMEM((2, 2, 4, 512, 128), BF),
            pltpu.VMEM((2, 4, 512, 128), BF), pltpu.VMEM((2, 2, 256, 128), BF), pltpu.VMEM((2, 2, 512, 128), BF),
            pltpu.VMEM((8, 128), F32), pltpu.VMEM((4, 8, 128), F32), pltpu.VMEM((4, 8, 128), F32), pltpu.VMEM((4, 8, 128), F32),
            D((8,)), D((8,)), D((2, 6)), D((2, 6)), D((2, 6)), D((2, 6)), D((10,)), D((10,)),
        ],
        compiler_params=pltpu.CompilerParams(collective_id=1, has_side_effects=True, vmem_limit_bytes=48 * 2 ** 20),
    )(slot, tile, g)


def attn(idx, kv_all, q, qT, do, doT):
    H = q.shape[0]
    V = functools.partial(pl.BlockSpec, memory_space=pltpu.VMEM)
    return pl.pallas_call(
        attn_kernel,
        out_shape=(
            jax.ShapeDtypeStruct((H, 512, 128), F32),
            jax.ShapeDtypeStruct((10, 512, 256), BF),
            jax.ShapeDtypeStruct((8, 128), F32),
        ),
        in_specs=[pl.BlockSpec(memory_space=pltpu.SMEM), pl.BlockSpec(memory_space=pl.ANY), V(), V(), V(), V()],
        out_specs=(V(), V(), V()),
        scratch_shapes=[
            pltpu.VMEM((9, 512, 128), BF), pltpu.VMEM((9, 512, 128), BF),
            pltpu.VMEM((9, 128, 512), BF), pltpu.VMEM((9, 128, 512), BF),
            pltpu.VMEM((2, 9, 512, 512), F32), pltpu.VMEM((2, 9, 512, 512), BF),
            pltpu.VMEM((9, 512, 128), F32), pltpu.VMEM((9, 512, 128), F32),
            pltpu.VMEM((128, 512), F32), pltpu.VMEM((128, 512), F32),
            pltpu.VMEM((2, 8, 512), F32), pltpu.VMEM((4, 8, 512), F32),
            pltpu.VMEM((2, 512, 128), BF), pltpu.VMEM((2, 512, 128), BF),
            pltpu.SemaphoreType.DMA((2, 9)),
        ],
        compiler_params=pltpu.CompilerParams(vmem_limit_bytes=60 * 2 ** 20),
    )(idx, kv_all, q, qT, do, doT)


def on_device(q_raw, k_raw, values, dout, q_gain, k_gain, chosen):
    blk, heads, width = q_raw.shape
    position = lax.axis_index("ctx")
    k2, v2 = k_raw.reshape(blk, width), values.reshape(blk, width)
    xk, rk, kn = norm_fwd(k2, k_gain)
    kv_all = lax.all_gather(jnp.concatenate([kn, v2], axis=1), "ctx", axis=0)
    xq, rq, qn = norm_fwd(jnp.transpose(q_raw, (1, 0, 2)), q_gain)
    do = jnp.transpose(dout, (1, 0, 2))
    idx = chosen.reshape(-1)
    dq, tile, kg = attn(idx, kv_all, qn, jnp.swapaxes(qn, 1, 2), do, jnp.swapaxes(do, 1, 2))
    dq_raw, gq = norm_back(xq, rq, q_gain, dq)
    part_q = jnp.sum(gq.reshape(-1, width), axis=0)
    part_k = jnp.sum(kg, axis=0) / k_gain
    target = jnp.concatenate([idx, position[None]])
    match = target[None, :] == jnp.arange(32, dtype=jnp.int32)[:, None]
    slot = jnp.min(jnp.where(match, jnp.arange(9, dtype=jnp.int32)[None, :], 9), axis=1)
    parts = jnp.concatenate([part_q[None], part_k[None], jnp.zeros((6, width), F32)], axis=0)
    dkn, dvalues, gains = scatter(slot, tile, parts)
    dk_raw, _ = norm_back(xk, rk, k_gain, dkn)
    return (
        jnp.transpose(dq_raw.astype(BF), (1, 0, 2)),
        dk_raw.astype(BF).reshape(blk, 1, width),
        dvalues.reshape(blk, 1, width),
        gains[0],
        gains[1],
    )


def solution(mesh):
    tok = P("ctx", "head", None)
    return jax.shard_map(
        on_device,
        mesh=mesh,
        in_specs=(tok, tok, tok, tok, P(), P(), tok),
        out_specs=(tok, tok, tok, P(), P()),
        check_vma=False,
    )
```

```python
import functools

import jax, jax.numpy as jnp
from jax import lax
from jax.experimental import pallas as pl
from jax.experimental.pallas import tpu as pltpu
from jax.sharding import PartitionSpec as P

SC = 128 ** -0.5
C2 = SC * 1.4426950408889634
NEG = -1e30
F32 = jnp.float32
BF = jnp.bfloat16

EPS = 1e-06


def norm_fwd(raw, gain):
    x = raw.astype(jnp.float32)
    scale_r = lax.rsqrt(jnp.mean(x * x, axis=-1, keepdims=True) + EPS)
    return (x, scale_r, (x * scale_r * gain).astype(jnp.bfloat16))


def norm_back(x, scale_r, gain, grad_y):
    along = gain * grad_y
    inner = jnp.mean(along * x, axis=-1, keepdims=True)
    grad_x = scale_r * (along - x * scale_r * scale_r * inner)
    return (grad_x, grad_y * x * scale_r)


def dot(a, b):
    return lax.dot_general(a, b, (((1,), (0,)), ((), ())), preferred_element_type=F32)

def fold(x, op):
    return op(x.reshape(x.shape[0] // 8, 8, x.shape[1]), axis=0)

def attn_kernel(idx_ref, kv_hbm, x_ref, q_ref, qT_ref, do_ref, doT_ref, qg_ref,
                dq_ref, tile_ref, kg_ref, gq_ref,
                kb, vb, kT, vT, S, E, dk, dv, oT, dqT, mrow, drow, qs, dos, dq32, sem):
    H = q_ref.shape[0]
    J = 9
    me = lax.axis_index("ctx")
    cps = []
    for j in range(J):
        blk = jnp.maximum(idx_ref[j], 0) if j < 8 else me
        cps.append((pltpu.make_async_copy(kv_hbm.at[blk, :, 0:128], kb.at[j], sem.at[0, j]),
                    pltpu.make_async_copy(kv_hbm.at[blk, :, 128:256], vb.at[j], sem.at[1, j])))
    for a, b in cps:
        a.start(); b.start()
    for a, b in cps:
        a.wait(); b.wait()

    kg_ref[...] = jnp.zeros(kg_ref.shape, F32)
    gq_ref[...] = jnp.zeros(gq_ref.shape, F32)
    tile_ref[J] = jnp.zeros(tile_ref.shape[1:], BF)

    rows = lax.broadcasted_iota(jnp.int32, (512, 512), 0)
    cols = lax.broadcasted_iota(jnp.int32, (512, 512), 1)

    def A1(h, j, own):
        s = dot(kb[j], qT_ref[h])
        if own:
            s = jnp.where(rows <= cols, s, NEG)
        S[j] = s
        cm = fold(s, jnp.max)
        if not own:
            cm = jnp.where(idx_ref[j] >= 0, cm, NEG)
        return cm

    def A2(h, j, own):
        m = mrow[h % 2]
        if not own:
            m = jnp.where(idx_ref[j] >= 0, m, 1e30)
        s = S[j]
        e = jnp.exp2((s.reshape(64, 8, 512) - m[None]) * C2)
        l = jnp.sum(e, axis=0)
        eb = e.reshape(512, 512).astype(BF)
        E[j] = eb
        oT[...] += dot(vT[j], eb)
        return l

    def C(h, j):
        dp = dot(vb[j], doT_ref[h])
        dl = drow[h % 2]
        dpb = (dp.reshape(64, 8, 512) - dl[None]).reshape(512, 512).astype(BF)
        eb = E[j]
        ds = eb * dpb
        dv[j] += dot(eb, dos[h % 2])
        dk[j] += dot(ds, qs[h % 2])
        dqT[...] += dot(kT[j], ds)

    def step(t, a1, a2, c):
        if a2:
            oT[...] = jnp.zeros(oT.shape, F32)
        if c:
            dqT[...] = jnp.zeros(dqT.shape, F32)

        def body(j, carry, own=False):
            mx, l = carry
            if a1 and not a2:
                vT[j] = vb[j].T
            if a1 and a2 and not c:
                kT[j] = kb[j].T
                dk[j] = jnp.zeros(dk.shape[1:], F32)
                dv[j] = jnp.zeros(dv.shape[1:], F32)
            if c:
                C(t - 2, j)
            if a2:
                l = l + A2(t - 1, j, own)
            if a1:
                mx = jnp.maximum(mx, A1(t, j, own))
            if c and not a2:
                kg_ref[...] += fold(dk[j] * kb[j].astype(F32), jnp.sum)
                tile_ref[j, :, 0:128] = dk[j].astype(BF)
                tile_ref[j, :, 128:256] = dv[j].astype(BF)
            return mx, l
        carry = (jnp.full((8, 512), NEG, F32), jnp.zeros((8, 512), F32))
        carry = lax.fori_loop(0, J - 1, body, carry, unroll=4)
        mx, l = body(J - 1, carry, True)
        if c:
            h = t - 2
            rl = drow[h % 2 + 2]
            dq = (dqT[...] * (rl[:1] * SC)).T
            x = x_ref[h].astype(F32)
            rq = lax.rsqrt(jnp.mean(x * x, axis=1, keepdims=True) + EPS)
            dq_raw, gq = norm_back(x, rq, qg_ref[...], dq)
            dq32[pl.ds(h, 512, stride=8), :] = dq_raw
            gq_ref[...] += fold(gq, jnp.sum)
        if a2:
            h = t - 1
            l1 = jnp.sum(l, axis=0, keepdims=True)
            rl = jnp.broadcast_to(1.0 / l1, (8, 512))
            o = oT[...]
            dl = jnp.sum(o * doT_ref[h].astype(F32), axis=0, keepdims=True) * rl[:1]
            drow[h % 2] = jnp.broadcast_to(dl, (8, 512))
            drow[h % 2 + 2] = rl
            rc = rl.T[:, :1]
            dos[h % 2] = (do_ref[h].astype(F32) * rc).astype(BF)
            qs[h % 2] = (q_ref[h].astype(F32) * (rc * SC)).astype(BF)
        if a1:
            m = jnp.max(mx, axis=0, keepdims=True)
            mrow[t % 2] = jnp.broadcast_to(m, (8, 512))

    step(0, True, False, False)
    step(1, True, True, False)

    @pl.loop(2, H)
    def _(t):
        step(t, True, True, True)
    step(H, False, True, True)
    step(H + 1, False, False, True)

    dq_ref[...] = dq32[...].astype(BF)


MESH = pl.DeviceIdType.MESH


def place():
    ctx, y = lax.axis_index("ctx"), lax.axis_index("head")
    return ctx // 8, (ctx // 2) % 4, ctx % 2, y


def peer(z, x, c, y):
    return (z * 8 + x * 2 + c, y)


def greet(devices):
    barrier = pltpu.get_barrier_semaphore()
    for d in devices:
        pl.semaphore_signal(barrier, inc=1, device_id=d, device_id_type=MESH)
    pl.semaphore_wait(barrier, len(devices))


def scatter_kernel(slot_ref, tile_ref, g_ref, dk_ref, dv_ref, gout_ref,
                   A, B, cur, R1, R2, T, Q1, Q2, GS, GZ, GX, GY,
                   s0, r0, s1, r1, s2, r2, sg, rg):
    z, x, c, y = place()

    def along(axis, off):
        if axis == "z":
            return peer((z + off) % 4, x, c, y)
        if axis == "x":
            return peer(z, (x + off) % 4, c, y)
        return peer(z, x, c, (y + off) % 4)

    sib = peer(z, x, 1 - c, y)
    greet([sib] + [along(a, o) for a in "zxy" for o in (1, 2, 3)])
    pending = []

    def send(src, dst, ss, rs, to):
        cp = pltpu.make_async_remote_copy(src_ref=src, dst_ref=dst, send_sem=ss, recv_sem=rs,
                                          device_id=to, device_id_type=MESH)
        cp.start()
        pending.append(cp)
        return cp

    gcp = send(g_ref, GS, sg.at[0], rg.at[0], sib)

    axes = (("z", "x"), ("x", "z"))
    coord = {"z": z, "x": x}

    def block(half, u, w, cc):
        return (u * 8 + w * 2 + cc) if half == 0 else (w * 8 + u * 2 + cc)

    def cols(half):
        return slice(half * 128, half * 128 + 128)

    first = {}
    for off in (2, 1, 3, 0):
        for half in (0, 1):
            u = (coord[axes[half][0]] + off) % 4

            @pl.loop(0, 4)
            def _(w):
                A[half, off, w] = tile_ref[slot_ref[block(half, u, w, 1 - c)], :, cols(half)]
            first[half, off] = send(A.at[half, off], B.at[half, off], s0.at[half * 4 + off], r0.at[half * 4 + off], sib)

    def group(G, base, kind):
        me = {"z": z, "x": x, "y": y}[kind]
        cps = [send(G.at[me], G.at[me], sg.at[base + o], rg.at[base + o], along(kind, o)) for o in (1, 2, 3)]
        return cps

    def gsum(G, cps):
        for cp in cps:
            cp.wait_recv()
        return (G[0] + G[1]) + (G[2] + G[3])

    def own_sum(half, off):
        first[half, off].wait_recv()
        u = (coord[axes[half][0]] + off) % 4

        @pl.loop(0, 4)
        def _(w):
            mine = tile_ref[slot_ref[block(half, u, w, c)], :, cols(half)]
            cur[half, off, w] = (mine.astype(F32) + B[half, off, w].astype(F32)).astype(BF)

    def s1send(k, half, src, dst, off):
        return send(src, dst, s1.at[half, k], r1.at[half, k], along(axes[half][0], off))

    c1 = {}
    for half in (0, 1):
        own_sum(half, 2)
        c1[half, 0] = s1send(0, half, cur.at[half, 2, 0:2], R1.at[half, 0], 1)
        c1[half, 1] = s1send(1, half, cur.at[half, 2, 2:4], R1.at[half, 1], 3)
    for half in (0, 1):
        own_sum(half, 1)
        c1[half, 2] = s1send(2, half, cur.at[half, 1, 2:4], R2.at[half, 0, 2:4], 1)
        own_sum(half, 3)
        c1[half, 3] = s1send(3, half, cur.at[half, 3, 0:2], R2.at[half, 1, 0:2], 3)
    gcp.wait_recv()
    GZ[z] = g_ref[...] + GS[...]
    gz = group(GZ, 0, "z")
    for half in (0, 1):
        own_sum(half, 0)
    for half in (0, 1):
        c1[half, 0].wait_recv()

        @pl.loop(0, 2)
        def _(w):
            cur[half, 1, w] = (cur[half, 1, w].astype(F32) + R1[half, 0, w].astype(F32)).astype(BF)
        c1[half, 4] = s1send(4, half, cur.at[half, 1, 0:2], R2.at[half, 0, 0:2], 1)
        c1[half, 1].wait_recv()

        @pl.loop(0, 2)
        def _(w):
            cur[half, 3, w + 2] = (cur[half, 3, w + 2].astype(F32) + R1[half, 1, w].astype(F32)).astype(BF)
        c1[half, 5] = s1send(5, half, cur.at[half, 3, 2:4], R2.at[half, 1, 2:4], 3)
    GX[x] = gsum(GZ, gz)
    gx = group(GX, 3, "x")

    def s2send(k, half, src, dst, off):
        return send(src, dst, s2.at[half, k], r2.at[half, k], along(axes[half][1], off))

    lo, hi = slice(0, 256), slice(256, 512)
    c2 = {}
    for half in (0, 1):
        for k in (2, 3, 4, 5):
            c1[half, k].wait_recv()
        cw = coord[axes[half][1]]

        @pl.loop(0, 4)
        def _(o):
            w = (cw + o) % 4
            T[half, o] = (cur[half, 0, w].astype(F32) + R2[half, 0, w].astype(F32)
                          + R2[half, 1, w].astype(F32)).astype(BF)
        c2[half, 0] = s2send(0, half, T.at[half, 2, lo], Q1.at[half, 0], 1)
        c2[half, 1] = s2send(1, half, T.at[half, 2, hi], Q1.at[half, 1], 3)
        c2[half, 2] = s2send(2, half, T.at[half, 1, hi], Q2.at[half, 0, hi], 1)
        c2[half, 3] = s2send(3, half, T.at[half, 3, lo], Q2.at[half, 1, lo], 3)
    GY[y] = gsum(GX, gx)
    gy = group(GY, 6, "y")
    for half in (0, 1):
        c2[half, 0].wait_recv()
        T[half, 1, lo] = (T[half, 1, lo].astype(F32) + Q1[half, 0].astype(F32)).astype(BF)
        c2[half, 4] = s2send(4, half, T.at[half, 1, lo], Q2.at[half, 0, lo], 1)
        c2[half, 1].wait_recv()
        T[half, 3, hi] = (T[half, 3, hi].astype(F32) + Q1[half, 1].astype(F32)).astype(BF)
        c2[half, 5] = s2send(5, half, T.at[half, 3, hi], Q2.at[half, 1, hi], 3)
    gout_ref[...] = gsum(GY, gy)
    for half in (0, 1):
        for k in (2, 3, 4, 5):
            c2[half, k].wait_recv()
        out = T[half, 0].astype(F32) + Q2[half, 0].astype(F32) + Q2[half, 1].astype(F32)
        if half == 0:
            dk_ref[...] = out
        else:
            dv_ref[...] = out.astype(BF)
    for cp in pending:
        cp.wait_send()


def scatter(slot, tile, g):
    V = functools.partial(pl.BlockSpec, memory_space=pltpu.VMEM)
    D = pltpu.SemaphoreType.DMA
    return pl.pallas_call(
        scatter_kernel,
        out_shape=(jax.ShapeDtypeStruct((512, 128), F32), jax.ShapeDtypeStruct((512, 128), BF),
                   jax.ShapeDtypeStruct((8, 128), F32)),
        in_specs=[pl.BlockSpec(memory_space=pltpu.SMEM), V(), V()],
        out_specs=(V(), V(), V()),
        scratch_shapes=[
            pltpu.VMEM((2, 4, 4, 512, 128), BF), pltpu.VMEM((2, 4, 4, 512, 128), BF), pltpu.VMEM((2, 4, 4, 512, 128), BF),
            pltpu.VMEM((2, 2, 2, 512, 128), BF), pltpu.VMEM((2, 2, 4, 512, 128), BF),
            pltpu.VMEM((2, 4, 512, 128), BF), pltpu.VMEM((2, 2, 256, 128), BF), pltpu.VMEM((2, 2, 512, 128), BF),
            pltpu.VMEM((8, 128), F32), pltpu.VMEM((4, 8, 128), F32), pltpu.VMEM((4, 8, 128), F32), pltpu.VMEM((4, 8, 128), F32),
            D((8,)), D((8,)), D((2, 6)), D((2, 6)), D((2, 6)), D((2, 6)), D((10,)), D((10,)),
        ],
        compiler_params=pltpu.CompilerParams(collective_id=1, has_side_effects=True, vmem_limit_bytes=48 * 2 ** 20),
    )(slot, tile, g)


def attn(idx, kv_all, x, q, qT, do, doT, qg):
    H = q.shape[0]
    V = functools.partial(pl.BlockSpec, memory_space=pltpu.VMEM)
    return pl.pallas_call(
        attn_kernel,
        out_shape=(
            jax.ShapeDtypeStruct((512 * H, 128), BF),
            jax.ShapeDtypeStruct((10, 512, 256), BF),
            jax.ShapeDtypeStruct((8, 128), F32),
            jax.ShapeDtypeStruct((8, 128), F32),
        ),
        in_specs=[pl.BlockSpec(memory_space=pltpu.SMEM), pl.BlockSpec(memory_space=pl.ANY), V(), V(), V(), V(), V(), V()],
        out_specs=(V(), V(), V(), V()),
        scratch_shapes=[
            pltpu.VMEM((9, 512, 128), BF), pltpu.VMEM((9, 512, 128), BF),
            pltpu.VMEM((9, 128, 512), BF), pltpu.VMEM((9, 128, 512), BF),
            pltpu.VMEM((9, 512, 512), F32), pltpu.VMEM((9, 512, 512), BF),
            pltpu.VMEM((9, 512, 128), F32), pltpu.VMEM((9, 512, 128), F32),
            pltpu.VMEM((128, 512), F32), pltpu.VMEM((128, 512), F32),
            pltpu.VMEM((2, 8, 512), F32), pltpu.VMEM((4, 8, 512), F32),
            pltpu.VMEM((2, 512, 128), BF), pltpu.VMEM((2, 512, 128), BF),
            pltpu.VMEM((512 * H, 128), F32),
            pltpu.SemaphoreType.DMA((2, 9)),
        ],
        compiler_params=pltpu.CompilerParams(vmem_limit_bytes=60 * 2 ** 20),
    )(idx, kv_all, x, q, qT, do, doT, qg)


def on_device(q_raw, k_raw, values, dout, q_gain, k_gain, chosen):
    blk, heads, width = q_raw.shape
    position = lax.axis_index("ctx")
    k2, v2 = k_raw.reshape(blk, width), values.reshape(blk, width)
    xk, rk, kn = norm_fwd(k2, k_gain)
    kv_all = lax.all_gather(jnp.concatenate([kn, v2], axis=1), "ctx", axis=0)
    xq = jnp.transpose(q_raw, (1, 0, 2))
    _, _, qn = norm_fwd(xq, q_gain)
    do = jnp.transpose(dout, (1, 0, 2))
    idx = chosen.reshape(-1)
    dq_raw, tile, kg, gq = attn(
        idx, kv_all, xq, qn, jnp.swapaxes(qn, 1, 2), do, jnp.swapaxes(do, 1, 2), q_gain[None])
    part_q = jnp.sum(gq, axis=0)
    part_k = jnp.sum(kg, axis=0) / k_gain
    target = jnp.concatenate([idx, position[None]])
    match = target[None, :] == jnp.arange(32, dtype=jnp.int32)[:, None]
    slot = jnp.min(jnp.where(match, jnp.arange(9, dtype=jnp.int32)[None, :], 9), axis=1)
    parts = jnp.concatenate([part_q[None], part_k[None], jnp.zeros((6, width), F32)], axis=0)
    dkn, dvalues, gains = scatter(slot, tile, parts)
    dk_raw, _ = norm_back(xk, rk, k_gain, dkn)
    return (
        dq_raw.reshape(blk, heads, width),
        dk_raw.astype(BF).reshape(blk, 1, width),
        dvalues.reshape(blk, 1, width),
        gains[0],
        gains[1],
    )


def solution(mesh):
    tok = P("ctx", "head", None)
    return jax.shard_map(
        on_device,
        mesh=mesh,
        in_specs=(tok, tok, tok, tok, P(), P(), tok),
        out_specs=(tok, tok, tok, P(), P()),
        check_vma=False,
    )
```

```python
import functools

import jax, jax.numpy as jnp
from jax import lax
from jax.experimental import pallas as pl
from jax.experimental.pallas import tpu as pltpu
from jax.sharding import PartitionSpec as P

SC = 128 ** -0.5
C2 = SC * 1.4426950408889634
NEG = -1e30
F32 = jnp.float32
BF = jnp.bfloat16

EPS = 1e-06


def norm_fwd(raw, gain):
    x = raw.astype(jnp.float32)
    scale_r = lax.rsqrt(jnp.mean(x * x, axis=-1, keepdims=True) + EPS)
    return (x, scale_r, (x * scale_r * gain).astype(jnp.bfloat16))


def norm_back(x, scale_r, gain, grad_y):
    along = gain * grad_y
    inner = jnp.mean(along * x, axis=-1, keepdims=True)
    grad_x = scale_r * (along - x * scale_r * scale_r * inner)
    return (grad_x, grad_y * x * scale_r)


def dot(a, b):
    return lax.dot_general(a, b, (((1,), (0,)), ((), ())), preferred_element_type=F32)

def fold(x, op):
    return op(x.reshape(x.shape[0] // 8, 8, x.shape[1]), axis=0)

def attn_kernel(idx_ref, kn_hbm, v_hbm, rows_hbm, cols_hbm, gain_ref,
                dq_ref, tile_ref, g_ref, rows_ref, cols_ref, kg_ref, gq_ref,
                kb, vb, kT, vT, S, E, dk, dv, oT, dqT, mrow, drow, qs, dos, dq32, sem, hsem):
    H = rows_hbm.shape[0]
    J = 9
    me = lax.axis_index("ctx")
    cps = []
    for j in range(J):
        blk = jnp.maximum(idx_ref[j], 0) if j < 8 else me
        cps.append((pltpu.make_async_copy(kn_hbm.at[blk], kb.at[j], sem.at[0, j]),
                    pltpu.make_async_copy(v_hbm.at[blk], vb.at[j], sem.at[1, j])))
    for a, b in cps:
        a.start(); b.start()

    def operands(h):
        return (pltpu.make_async_copy(rows_hbm.at[h], rows_ref.at[h], hsem.at[0, h]),
                pltpu.make_async_copy(cols_hbm.at[h], cols_ref.at[h], hsem.at[1, h]))

    for h in range(H):
        for cp in operands(h):
            cp.start()
    for a, b in cps:
        a.wait(); b.wait()

    kg_ref[...] = jnp.zeros(kg_ref.shape, F32)
    gq_ref[...] = jnp.zeros(gq_ref.shape, F32)
    tile_ref[J] = jnp.zeros(tile_ref.shape[1:], BF)

    rows = lax.broadcasted_iota(jnp.int32, (512, 512), 0)
    cols = lax.broadcasted_iota(jnp.int32, (512, 512), 1)

    def A1(h, j, own):
        s = dot(kb[j], cols_ref[h, 0])
        if own:
            s = jnp.where(rows <= cols, s, NEG)
        S[j] = s
        cm = fold(s, jnp.max)
        if not own:
            cm = jnp.where(idx_ref[j] >= 0, cm, NEG)
        return cm

    def A2(h, j, own):
        m = mrow[h % 2]
        if not own:
            m = jnp.where(idx_ref[j] >= 0, m, 1e30)
        s = S[j]
        e = jnp.exp2((s.reshape(64, 8, 512) - m[None]) * C2)
        l = jnp.sum(e, axis=0)
        eb = e.reshape(512, 512).astype(BF)
        E[j] = eb
        oT[...] += dot(vT[j], eb)
        return l

    def C(h, j):
        dp = dot(vb[j], cols_ref[h, 1])
        dl = drow[h % 2]
        dpb = (dp.reshape(64, 8, 512) - dl[None]).reshape(512, 512).astype(BF)
        eb = E[j]
        ds = eb * dpb
        dv[j] += dot(eb, dos[h % 2])
        dk[j] += dot(ds, qs[h % 2])
        dqT[...] += dot(kT[j], ds)

    def step(t, a1, a2, c):
        if a1:
            for cp in operands(t):
                cp.wait()
        if a2:
            oT[...] = jnp.zeros(oT.shape, F32)
        if c:
            dqT[...] = jnp.zeros(dqT.shape, F32)

        def body(j, carry, own=False):
            mx, l = carry
            if a1 and not a2:
                vT[j] = vb[j].T
            if a1 and a2 and not c:
                kT[j] = kb[j].T
                dk[j] = jnp.zeros(dk.shape[1:], F32)
                dv[j] = jnp.zeros(dv.shape[1:], F32)
            if c:
                C(t - 2, j)
            if a2:
                l = l + A2(t - 1, j, own)
            if a1:
                mx = jnp.maximum(mx, A1(t, j, own))
            if c and not a2:
                kg_ref[...] += fold(dk[j] * kb[j].astype(F32), jnp.sum)
                tile_ref[j, :, 0:128] = dk[j].astype(BF)
                tile_ref[j, :, 128:256] = dv[j].astype(BF)
            return mx, l
        carry = (jnp.full((8, 512), NEG, F32), jnp.zeros((8, 512), F32))
        carry = lax.fori_loop(0, J - 1, body, carry, unroll=4)
        mx, l = body(J - 1, carry, True)
        if c:
            h = t - 2
            rl = drow[h % 2 + 2]
            dq = (dqT[...] * (rl[:1] * SC)).T
            x = rows_ref[h, 0].astype(F32)
            rq = lax.rsqrt(jnp.mean(x * x, axis=1, keepdims=True) + EPS)
            dq_raw, gq = norm_back(x, rq, gain_ref[0:1], dq)
            dq32[pl.ds(h, 512, stride=8), :] = dq_raw
            gq_ref[...] += fold(gq, jnp.sum)
        if a2:
            h = t - 1
            l1 = jnp.sum(l, axis=0, keepdims=True)
            rl = jnp.broadcast_to(1.0 / l1, (8, 512))
            o = oT[...]
            dl = jnp.sum(o * cols_ref[h, 1].astype(F32), axis=0, keepdims=True) * rl[:1]
            drow[h % 2] = jnp.broadcast_to(dl, (8, 512))
            drow[h % 2 + 2] = rl
            rc = rl.T[:, :1]
            dos[h % 2] = (rows_ref[h, 2].astype(F32) * rc).astype(BF)
            qs[h % 2] = (rows_ref[h, 1].astype(F32) * (rc * SC)).astype(BF)
        if a1:
            m = jnp.max(mx, axis=0, keepdims=True)
            mrow[t % 2] = jnp.broadcast_to(m, (8, 512))

    step(0, True, False, False)
    step(1, True, True, False)

    @pl.loop(2, H)
    def _(t):
        step(t, True, True, True)
    step(H, False, True, True)
    step(H + 1, False, False, True)

    dq_ref[...] = dq32[...].astype(BF)
    part_q = jnp.sum(gq_ref[...], axis=0, keepdims=True)
    part_k = jnp.sum(kg_ref[...], axis=0, keepdims=True) / gain_ref[1:2]
    row = lax.broadcasted_iota(jnp.int32, (8, 128), 0)
    g_ref[...] = jnp.where(row == 0, part_q, jnp.where(row == 1, part_k, 0.0))


MESH = pl.DeviceIdType.MESH


def place():
    ctx, y = lax.axis_index("ctx"), lax.axis_index("head")
    return ctx // 8, (ctx // 2) % 4, ctx % 2, y


def peer(z, x, c, y):
    return (z * 8 + x * 2 + c, y)


def greet(devices):
    barrier = pltpu.get_barrier_semaphore()
    for d in devices:
        pl.semaphore_signal(barrier, inc=1, device_id=d, device_id_type=MESH)
    pl.semaphore_wait(barrier, len(devices))


def scatter_kernel(slot_ref, tile_hbm, g_ref, dk_ref, dv_ref, gout_ref,
                   tile_ref, tsem, A, B, cur, R1, R2, T, Q1, Q2, GS, GZ, GX, GY,
                   s0, r0, s1, r1, s2, r2, sg, rg):
    z, x, c, y = place()

    def along(axis, off):
        if axis == "z":
            return peer((z + off) % 4, x, c, y)
        if axis == "x":
            return peer(z, (x + off) % 4, c, y)
        return peer(z, x, c, (y + off) % 4)

    fetch = pltpu.make_async_copy(tile_hbm, tile_ref, tsem)
    fetch.start()
    sib = peer(z, x, 1 - c, y)
    greet([sib] + [along(a, o) for a in "zxy" for o in (1, 2, 3)])
    pending = []

    def send(src, dst, ss, rs, to):
        cp = pltpu.make_async_remote_copy(src_ref=src, dst_ref=dst, send_sem=ss, recv_sem=rs,
                                          device_id=to, device_id_type=MESH)
        cp.start()
        pending.append(cp)
        return cp

    fetch.wait()
    gcp = send(g_ref, GS, sg.at[0], rg.at[0], sib)

    axes = (("z", "x"), ("x", "z"))
    coord = {"z": z, "x": x}

    def block(half, u, w, cc):
        return (u * 8 + w * 2 + cc) if half == 0 else (w * 8 + u * 2 + cc)

    def cols(half):
        return slice(half * 128, half * 128 + 128)

    first = {}
    for off in (2, 1, 3, 0):
        for half in (0, 1):
            u = (coord[axes[half][0]] + off) % 4

            @pl.loop(0, 4)
            def _(w):
                A[half, off, w] = tile_ref[slot_ref[block(half, u, w, 1 - c)], :, cols(half)]
            first[half, off] = send(A.at[half, off], B.at[half, off], s0.at[half * 4 + off], r0.at[half * 4 + off], sib)

    def group(G, base, kind):
        me = {"z": z, "x": x, "y": y}[kind]
        cps = [send(G.at[me], G.at[me], sg.at[base + o], rg.at[base + o], along(kind, o)) for o in (1, 2, 3)]
        return cps

    def gsum(G, cps):
        for cp in cps:
            cp.wait_recv()
        return (G[0] + G[1]) + (G[2] + G[3])

    def own_sum(half, off):
        first[half, off].wait_recv()
        u = (coord[axes[half][0]] + off) % 4

        @pl.loop(0, 4)
        def _(w):
            mine = tile_ref[slot_ref[block(half, u, w, c)], :, cols(half)]
            cur[half, off, w] = (mine.astype(F32) + B[half, off, w].astype(F32)).astype(BF)

    def s1send(k, half, src, dst, off):
        return send(src, dst, s1.at[half, k], r1.at[half, k], along(axes[half][0], off))

    c1 = {}
    for half in (0, 1):
        own_sum(half, 2)
        c1[half, 0] = s1send(0, half, cur.at[half, 2, 0:2], R1.at[half, 0], 1)
        c1[half, 1] = s1send(1, half, cur.at[half, 2, 2:4], R1.at[half, 1], 3)
    for half in (0, 1):
        own_sum(half, 1)
        c1[half, 2] = s1send(2, half, cur.at[half, 1, 2:4], R2.at[half, 0, 2:4], 1)
        own_sum(half, 3)
        c1[half, 3] = s1send(3, half, cur.at[half, 3, 0:2], R2.at[half, 1, 0:2], 3)
    gcp.wait_recv()
    GZ[z] = g_ref[...] + GS[...]
    gz = group(GZ, 0, "z")
    for half in (0, 1):
        own_sum(half, 0)
    for half in (0, 1):
        c1[half, 0].wait_recv()

        @pl.loop(0, 2)
        def _(w):
            cur[half, 1, w] = (cur[half, 1, w].astype(F32) + R1[half, 0, w].astype(F32)).astype(BF)
        c1[half, 4] = s1send(4, half, cur.at[half, 1, 0:2], R2.at[half, 0, 0:2], 1)
        c1[half, 1].wait_recv()

        @pl.loop(0, 2)
        def _(w):
            cur[half, 3, w + 2] = (cur[half, 3, w + 2].astype(F32) + R1[half, 1, w].astype(F32)).astype(BF)
        c1[half, 5] = s1send(5, half, cur.at[half, 3, 2:4], R2.at[half, 1, 2:4], 3)
    GX[x] = gsum(GZ, gz)
    gx = group(GX, 3, "x")

    def s2send(k, half, src, dst, off):
        return send(src, dst, s2.at[half, k], r2.at[half, k], along(axes[half][1], off))

    lo, hi = slice(0, 256), slice(256, 512)
    c2 = {}
    for half in (0, 1):
        for k in (2, 3, 4, 5):
            c1[half, k].wait_recv()
        cw = coord[axes[half][1]]

        @pl.loop(0, 4)
        def _(o):
            w = (cw + o) % 4
            T[half, o] = (cur[half, 0, w].astype(F32) + R2[half, 0, w].astype(F32)
                          + R2[half, 1, w].astype(F32)).astype(BF)
        c2[half, 0] = s2send(0, half, T.at[half, 2, lo], Q1.at[half, 0], 1)
        c2[half, 1] = s2send(1, half, T.at[half, 2, hi], Q1.at[half, 1], 3)
        c2[half, 2] = s2send(2, half, T.at[half, 1, hi], Q2.at[half, 0, hi], 1)
        c2[half, 3] = s2send(3, half, T.at[half, 3, lo], Q2.at[half, 1, lo], 3)
    GY[y] = gsum(GX, gx)
    gy = group(GY, 6, "y")
    for half in (0, 1):
        c2[half, 0].wait_recv()
        T[half, 1, lo] = (T[half, 1, lo].astype(F32) + Q1[half, 0].astype(F32)).astype(BF)
        c2[half, 4] = s2send(4, half, T.at[half, 1, lo], Q2.at[half, 0, lo], 1)
        c2[half, 1].wait_recv()
        T[half, 3, hi] = (T[half, 3, hi].astype(F32) + Q1[half, 1].astype(F32)).astype(BF)
        c2[half, 5] = s2send(5, half, T.at[half, 3, hi], Q2.at[half, 1, hi], 3)
    gout_ref[...] = gsum(GY, gy)
    for half in (0, 1):
        for k in (2, 3, 4, 5):
            c2[half, k].wait_recv()
        out = T[half, 0].astype(F32) + Q2[half, 0].astype(F32) + Q2[half, 1].astype(F32)
        if half == 0:
            dk_ref[...] = out
        else:
            dv_ref[...] = out.astype(BF)
    for cp in pending:
        cp.wait_send()


def scatter(slot, tile, g):
    V = functools.partial(pl.BlockSpec, memory_space=pltpu.VMEM)
    D = pltpu.SemaphoreType.DMA
    return pl.pallas_call(
        scatter_kernel,
        out_shape=(jax.ShapeDtypeStruct((512, 128), F32), jax.ShapeDtypeStruct((512, 128), BF),
                   jax.ShapeDtypeStruct((8, 128), F32)),
        in_specs=[pl.BlockSpec(memory_space=pltpu.SMEM), pl.BlockSpec(memory_space=pl.ANY), V()],
        out_specs=(V(), V(), V()),
        scratch_shapes=[
            pltpu.VMEM((10, 512, 256), BF), D(()),
            pltpu.VMEM((2, 4, 4, 512, 128), BF), pltpu.VMEM((2, 4, 4, 512, 128), BF), pltpu.VMEM((2, 4, 4, 512, 128), BF),
            pltpu.VMEM((2, 2, 2, 512, 128), BF), pltpu.VMEM((2, 2, 4, 512, 128), BF),
            pltpu.VMEM((2, 4, 512, 128), BF), pltpu.VMEM((2, 2, 256, 128), BF), pltpu.VMEM((2, 2, 512, 128), BF),
            pltpu.VMEM((8, 128), F32), pltpu.VMEM((4, 8, 128), F32), pltpu.VMEM((4, 8, 128), F32), pltpu.VMEM((4, 8, 128), F32),
            D((8,)), D((8,)), D((2, 6)), D((2, 6)), D((2, 6)), D((2, 6)), D((10,)), D((10,)),
        ],
        compiler_params=pltpu.CompilerParams(collective_id=1, has_side_effects=True, vmem_limit_bytes=60 * 2 ** 20),
    )(slot, tile, g)


def gather_kernel(k_ref, v_ref, q_ref, do_ref, gain_ref, ko_ref, vo_ref, rows_out, cols_out,
                  kn_ref, q32, do32, rows, cols, lsem, psem, ss, rs):
    z, x, c, y = place()

    def along(axis, off):
        return peer((z + off) % 4, x, c, y) if axis == "z" else peer(z, (x + off) % 4, c, y)

    _, _, kn = norm_fwd(k_ref[...], gain_ref[1:2])
    kn_ref[...] = kn
    sib = peer(z, x, 1 - c, y)
    greet([sib] + [along(a, o) for a in "zx" for o in (1, 3)])
    coord = {"z": z, "x": x}
    pending = []
    sibling = []
    count = [0, 0]

    halves = ((kn_ref, ko_ref, "x", "z"), (v_ref, vo_ref, "z", "x"))
    lo, hi, full = slice(0, 256), slice(256, 512), slice(0, 512)

    def block(half, uo, wo, cc=None):
        cc = c if cc is None else cc
        u = (coord[halves[half][2]] + uo) % 4
        w = (coord[halves[half][3]] + wo) % 4
        return u * 2 + w * 8 + cc if half == 0 else u * 8 + w * 2 + cc

    def send(half, uo, wo, rows, to, src=None):
        out = halves[half][1]
        k = count[half]
        count[half] += 1
        b = block(half, uo, wo)
        cp = pltpu.make_async_remote_copy(
            src_ref=out.at[b, rows] if src is None else src, dst_ref=out.at[b, rows],
            send_sem=ss.at[half, k], recv_sem=rs.at[half, k], device_id=to, device_id_type=MESH)
        cp.start()
        pending.append(cp)
        return cp

    local = []
    for half, (src, out, u, w) in enumerate(halves):
        cp = pltpu.make_async_copy(src, out.at[block(half, 0, 0)], lsem.at[half])
        cp.start()
        local.append(cp)
    got = {}
    for half, (src, out, u, w) in enumerate(halves):
        got[half, "u+"] = send(half, 0, 0, full, along(u, 1), src)
        got[half, "u-"] = send(half, 0, 0, full, along(u, 3), src)
    q32[...] = q_ref[...].astype(F32)
    do32[...] = do_ref[...].astype(F32)

    def prep(h):
        x = q32[pl.ds(h, 512, stride=8), :]
        _, _, qn = norm_fwd(x, gain_ref[0:1])
        d = do32[pl.ds(h, 512, stride=8), :].astype(BF)
        rows[h, 0] = x.astype(BF)
        rows[h, 1] = qn
        rows[h, 2] = d
        cols[h, 0] = qn.T
        cols[h, 1] = d.T
        for n, (src, dst) in enumerate(((rows, rows_out), (cols, cols_out))):
            cp = pltpu.make_async_copy(src.at[h], dst.at[h], psem.at[n, h])
            cp.start()
            local.append(cp)

    for half, (src, out, u, w) in enumerate(halves):
        got[half, 0, "w+"] = send(half, 0, 0, full, along(w, 1), src)
        got[half, 0, "w-"] = send(half, 0, 0, full, along(w, 3), src)
        sibling.append(send(half, 0, 0, full, sib, src))
    prep(0)
    for half, (src, out, u, w) in enumerate(halves):
        got[half, "u+"].wait_recv()
        got[half, "f+"] = send(half, 3, 0, lo, along(u, 1))
        got[half, 3, "w+"] = send(half, 3, 0, full, along(w, 1))
        got[half, 3, "w-"] = send(half, 3, 0, full, along(w, 3))
        sibling.append(send(half, 3, 0, full, sib))
        got[half, "u-"].wait_recv()
        got[half, "f-"] = send(half, 1, 0, hi, along(u, 3))
        got[half, 1, "w+"] = send(half, 1, 0, full, along(w, 1))
        got[half, 1, "w-"] = send(half, 1, 0, full, along(w, 3))
        sibling.append(send(half, 1, 0, full, sib))

    def onward(half, uo):
        w = halves[half][3]
        got[half, uo, "w+"].wait_recv()
        got[half, uo, "g+"] = send(half, uo, 3, lo, along(w, 1))
        sibling.append(send(half, uo, 3, full, sib))
        got[half, uo, "w-"].wait_recv()
        got[half, uo, "g-"] = send(half, uo, 1, hi, along(w, 3))
        sibling.append(send(half, uo, 1, full, sib))

    prep(1)
    for half in (0, 1):
        onward(half, 0)
    prep(2)
    for half, (src, out, u, w) in enumerate(halves):
        got[half, "f+"].wait_recv()
        got[half, "f-"].wait_recv()
        got[half, 2, "w+"] = send(half, 2, 0, full, along(w, 1))
        got[half, 2, "w-"] = send(half, 2, 0, full, along(w, 3))
        sibling.append(send(half, 2, 0, full, sib))
    for uo in (3, 1, 2):
        prep(3 + (uo % 3))
        for half in (0, 1):
            onward(half, uo)
    prep(6)
    prep(7)
    for uo in (0, 3, 1, 2):
        for half in (0, 1):
            got[half, uo, "g+"].wait_recv()
            got[half, uo, "g-"].wait_recv()
            sibling.append(send(half, uo, 2, full, sib))
    for cp in sibling:
        cp.wait_recv()
    for cp in pending:
        cp.wait_send()
    for cp in local:
        cp.wait()


def gather(k, v, q, do, gains):
    D = pltpu.SemaphoreType.DMA
    anys = pl.BlockSpec(memory_space=pl.ANY)
    vm = pl.BlockSpec(memory_space=pltpu.VMEM)
    return pl.pallas_call(
        gather_kernel,
        out_shape=(jax.ShapeDtypeStruct((32, 512, 128), BF), jax.ShapeDtypeStruct((32, 512, 128), BF),
                   jax.ShapeDtypeStruct((8, 3, 512, 128), BF), jax.ShapeDtypeStruct((8, 2, 128, 512), BF)),
        in_specs=[vm] * 5,
        out_specs=(anys,) * 4,
        scratch_shapes=[
            pltpu.VMEM((512, 128), BF), pltpu.VMEM((4096, 128), F32), pltpu.VMEM((4096, 128), F32),
            pltpu.VMEM((8, 3, 512, 128), BF), pltpu.VMEM((8, 2, 128, 512), BF),
            D((2,)), D((2, 8)), D((2, 36)), D((2, 36)),
        ],
        compiler_params=pltpu.CompilerParams(collective_id=0, has_side_effects=True, vmem_limit_bytes=60 * 2 ** 20),
    )(k, v, q, do, gains)


def attn(idx, kn_all, v_all, rows, cols, gains):
    H = rows.shape[0]
    V = functools.partial(pl.BlockSpec, memory_space=pltpu.VMEM)
    A = functools.partial(pl.BlockSpec, memory_space=pl.ANY)
    return pl.pallas_call(
        attn_kernel,
        out_shape=(
            jax.ShapeDtypeStruct((512 * H, 128), BF),
            jax.ShapeDtypeStruct((10, 512, 256), BF),
            jax.ShapeDtypeStruct((8, 128), F32),
        ),
        in_specs=[pl.BlockSpec(memory_space=pltpu.SMEM), A(), A(), A(), A(), V()],
        out_specs=(V(), V(), V()),
        scratch_shapes=[
            pltpu.VMEM((H, 3, 512, 128), BF), pltpu.VMEM((H, 2, 128, 512), BF),
            pltpu.VMEM((8, 128), F32), pltpu.VMEM((8, 128), F32),
            pltpu.VMEM((9, 512, 128), BF), pltpu.VMEM((9, 512, 128), BF),
            pltpu.VMEM((9, 128, 512), BF), pltpu.VMEM((9, 128, 512), BF),
            pltpu.VMEM((9, 512, 512), F32), pltpu.VMEM((9, 512, 512), BF),
            pltpu.VMEM((9, 512, 128), F32), pltpu.VMEM((9, 512, 128), F32),
            pltpu.VMEM((128, 512), F32), pltpu.VMEM((128, 512), F32),
            pltpu.VMEM((2, 8, 512), F32), pltpu.VMEM((4, 8, 512), F32),
            pltpu.VMEM((2, 512, 128), BF), pltpu.VMEM((2, 512, 128), BF),
            pltpu.VMEM((512 * H, 128), F32),
            pltpu.SemaphoreType.DMA((2, 9)), pltpu.SemaphoreType.DMA((2, H)),
        ],
        compiler_params=pltpu.CompilerParams(vmem_limit_bytes=60 * 2 ** 20),
    )(idx, kn_all, v_all, rows, cols, gains)


def on_device(q_raw, k_raw, values, dout, q_gain, k_gain, chosen):
    blk, heads, width = q_raw.shape
    position = lax.axis_index("ctx")
    k2, v2 = k_raw.reshape(blk, width), values.reshape(blk, width)
    gains = jnp.concatenate([q_gain[None], k_gain[None], jnp.ones((6, width), F32)], axis=0)
    kn_all, v_all, rows, cols = gather(
        k2, v2, q_raw.reshape(blk * heads, width), dout.reshape(blk * heads, width), gains)
    idx = chosen.reshape(-1)
    dq_raw, tile, parts = attn(idx, kn_all, v_all, rows, cols, gains)
    target = jnp.concatenate([idx, position[None]])
    match = target[None, :] == jnp.arange(32, dtype=jnp.int32)[:, None]
    slot = jnp.min(jnp.where(match, jnp.arange(9, dtype=jnp.int32)[None, :], 9), axis=1)
    dkn, dvalues, sums = scatter(slot, tile, parts)
    xk, rk, _ = norm_fwd(k2, k_gain)
    dk_raw, _ = norm_back(xk, rk, k_gain, dkn)
    return (
        dq_raw.reshape(blk, heads, width),
        dk_raw.astype(BF).reshape(blk, 1, width),
        dvalues.reshape(blk, 1, width),
        sums[0],
        sums[1],
    )


def solution(mesh):
    tok = P("ctx", "head", None)
    return jax.shard_map(
        on_device,
        mesh=mesh,
        in_specs=(tok, tok, tok, tok, P(), P(), tok),
        out_specs=(tok, tok, tok, P(), P()),
        check_vma=False,
    )
```

```python
import functools

import jax, jax.numpy as jnp
from jax import lax
from jax.experimental import pallas as pl
from jax.experimental.pallas import tpu as pltpu
from jax.sharding import PartitionSpec as P

SC = 128 ** -0.5
C2 = SC * 1.4426950408889634
NEG = -1e30
F32 = jnp.float32
BF = jnp.bfloat16

EPS = 1e-06


def norm_fwd(raw, gain):
    x = raw.astype(jnp.float32)
    scale_r = lax.rsqrt(jnp.mean(x * x, axis=-1, keepdims=True) + EPS)
    return (x, scale_r, (x * scale_r * gain).astype(jnp.bfloat16))


def norm_back(x, scale_r, gain, grad_y):
    along = gain * grad_y
    inner = jnp.mean(along * x, axis=-1, keepdims=True)
    grad_x = scale_r * (along - x * scale_r * scale_r * inner)
    return (grad_x, grad_y * x * scale_r)


def dot(a, b):
    return lax.dot_general(a, b, (((1,), (0,)), ((), ())), preferred_element_type=F32)

def fold(x, op):
    return op(x.reshape(x.shape[0] // 8, 8, x.shape[1]), axis=0)

def attn_kernel(idx_ref, kn_hbm, v_hbm, rows_hbm, cols_hbm, qgain_ref, kgain_ref,
                dq_ref, tile_hbm, g_ref, slot_ref, tile_ref, rows_ref, cols_ref, kg_ref, gq_ref,
                kb, vb, kT, S, DP, E, dk, dv, dqT, mrow, drow, qs, dos, dq32, sem, hsem):
    H = rows_hbm.shape[0]
    J = 9
    me = lax.axis_index("ctx")
    def operand(j, own, n):
        blk = me if own else jnp.maximum(idx_ref[j], 0)
        src, dst = ((kn_hbm, kb), (v_hbm, vb))[n]
        return pltpu.make_async_copy(src.at[blk], dst.at[j], sem.at[n, j])

    def tile_out(j):
        return pltpu.make_async_copy(tile_ref.at[j], tile_hbm.at[j], sem.at[2, j])

    def operands(h):
        return (pltpu.make_async_copy(rows_hbm.at[h], rows_ref.at[h], hsem.at[0, h]),
                pltpu.make_async_copy(cols_hbm.at[h], cols_ref.at[h], hsem.at[1, h]))

    for cp in operands(0):
        cp.start()
    for n in (0, 1):
        for j in range(J):
            operand(j, j == J - 1, n).start()
    for h in range(1, H):
        for cp in operands(h):
            cp.start()
    for b in range(40):
        slot_ref[b] = J
    for j in range(J - 1):
        slot_ref[jnp.where(idx_ref[j] >= 0, idx_ref[j], 32)] = j
    slot_ref[me] = J - 1
    kg_ref[...] = jnp.zeros(kg_ref.shape, F32)
    gq_ref[...] = jnp.zeros(gq_ref.shape, F32)
    tile_ref[J] = jnp.zeros(tile_ref.shape[1:], BF)
    tile_out(J).start()

    rows = lax.broadcasted_iota(jnp.int32, (512, 512), 0)
    cols = lax.broadcasted_iota(jnp.int32, (512, 512), 1)

    def A1(h, j, own):
        s = dot(kb[j], cols_ref[h, 0])
        if own:
            s = jnp.where(rows <= cols, s, NEG)
        S[j] = s
        cm = fold(s, jnp.max)
        if not own:
            cm = jnp.where(idx_ref[j] >= 0, cm, NEG)
        return cm

    def A2(h, j, own):
        m = mrow[h % 2]
        if not own:
            m = jnp.where(idx_ref[j] >= 0, m, 1e30)
        s = S[j]
        e = jnp.exp2((s.reshape(64, 8, 512) - m[None]) * C2)
        l = jnp.sum(e, axis=0)
        eb = e.reshape(512, 512).astype(BF)
        E[j] = eb
        dp = dot(vb[j], cols_ref[h, 1])
        DP[j] = dp
        return l, fold(e.reshape(512, 512) * dp, jnp.sum)

    def C(h, j):
        dp = DP[j]
        dl = drow[h % 2]
        dpb = (dp.reshape(64, 8, 512) - dl[None]).reshape(512, 512).astype(BF)
        eb = E[j]
        ds = eb * dpb
        dv[j] += dot(eb, dos[h % 2])
        dk[j] += dot(ds, qs[h % 2])
        dqT[...] += dot(kT[j], ds)

    def step(t, a1, a2, c):
        if a1:
            for cp in operands(t):
                cp.wait()
        if c:
            dqT[...] = jnp.zeros(dqT.shape, F32)

        def body(j, carry, own=False):
            mx, l, dd = carry
            if a1 and not a2:
                operand(j, own, 0).wait()
            if a1 and a2 and not c:
                operand(j, own, 1).wait()
                kT[j] = kb[j].T
                dk[j] = jnp.zeros(dk.shape[1:], F32)
                dv[j] = jnp.zeros(dv.shape[1:], F32)
            if c:
                C(t - 2, j)
            if a2:
                l_j, d_j = A2(t - 1, j, own)
                l, dd = l + l_j, dd + d_j
            if a1:
                mx = jnp.maximum(mx, A1(t, j, own))
            if c and not a2:
                kg_ref[...] += fold(dk[j] * kb[j].astype(F32), jnp.sum)
                tile_ref[j, :, 0:128] = dk[j].astype(BF)
                tile_ref[j, :, 128:256] = dv[j].astype(BF)
                tile_out(j).start()
            return mx, l, dd
        carry = (jnp.full((8, 512), NEG, F32), jnp.zeros((8, 512), F32), jnp.zeros((8, 512), F32))
        carry = lax.fori_loop(0, J - 1, body, carry, unroll=8)
        mx, l, dd = body(J - 1, carry, True)
        if c:
            h = t - 2
            rl = drow[h % 2 + 2]
            dq = (dqT[...] * (rl[:1] * SC)).T
            x = rows_ref[h, 0].astype(F32)
            rq = lax.rsqrt(jnp.mean(x * x, axis=1, keepdims=True) + EPS)
            dq_raw, gq = norm_back(x, rq, qgain_ref[...], dq)
            dq32[pl.ds(h, 512, stride=8), :] = dq_raw
            gq_ref[...] += fold(gq, jnp.sum)
        if a2:
            h = t - 1
            l1 = jnp.sum(l, axis=0, keepdims=True)
            rl = jnp.broadcast_to(1.0 / l1, (8, 512))
            dl = jnp.sum(dd, axis=0, keepdims=True) * rl[:1]
            drow[h % 2] = jnp.broadcast_to(dl, (8, 512))
            drow[h % 2 + 2] = rl
            rc = rl.T[:, :1]
            dos[h % 2] = (rows_ref[h, 2].astype(F32) * rc).astype(BF)
            qs[h % 2] = (rows_ref[h, 1].astype(F32) * (rc * SC)).astype(BF)
        if a1:
            m = jnp.max(mx, axis=0, keepdims=True)
            mrow[t % 2] = jnp.broadcast_to(m, (8, 512))

    step(0, True, False, False)
    step(1, True, True, False)

    @pl.loop(2, H)
    def _(t):
        step(t, True, True, True)
    step(H, False, True, True)
    step(H + 1, False, False, True)

    dq_ref[...] = dq32[...].astype(BF)
    part_q = jnp.sum(gq_ref[...], axis=0, keepdims=True)
    part_k = jnp.sum(kg_ref[...], axis=0, keepdims=True) / kgain_ref[...]
    row = lax.broadcasted_iota(jnp.int32, (8, 128), 0)
    g_ref[...] = jnp.where(row == 0, part_q, jnp.where(row == 1, part_k, 0.0))
    for j in range(J + 1):
        tile_out(j).wait()


MESH = pl.DeviceIdType.MESH


def place():
    ctx, y = lax.axis_index("ctx"), lax.axis_index("head")
    return ctx // 8, (ctx // 2) % 4, ctx % 2, y


def peer(z, x, c, y):
    return (z * 8 + x * 2 + c, y)


def greet(devices):
    barrier = pltpu.get_barrier_semaphore()
    for d in devices:
        pl.semaphore_signal(barrier, inc=1, device_id=d, device_id_type=MESH)
    pl.semaphore_wait(barrier, len(devices))


def scatter_kernel(slot_ref, tile_hbm, g_ref, dk_ref, dv_ref, gout_ref,
                   tile_ref, tsem, A, B, cur, R1, R2, T, Q1, Q2, GS, GZ, GX, GY,
                   s0, r0, s1, r1, s2, r2, sg, rg):
    z, x, c, y = place()

    def along(axis, off):
        if axis == "z":
            return peer((z + off) % 4, x, c, y)
        if axis == "x":
            return peer(z, (x + off) % 4, c, y)
        return peer(z, x, c, (y + off) % 4)

    fetch = pltpu.make_async_copy(tile_hbm, tile_ref, tsem)
    fetch.start()
    sib = peer(z, x, 1 - c, y)
    greet([sib] + [along(a, o) for a in "zxy" for o in (1, 2, 3)])
    pending = []

    def send(src, dst, ss, rs, to):
        cp = pltpu.make_async_remote_copy(src_ref=src, dst_ref=dst, send_sem=ss, recv_sem=rs,
                                          device_id=to, device_id_type=MESH)
        cp.start()
        pending.append(cp)
        return cp

    fetch.wait()
    gcp = send(g_ref, GS, sg.at[0], rg.at[0], sib)

    axes = (("z", "x"), ("x", "z"))
    coord = {"z": z, "x": x}

    def block(half, u, w, cc):
        return (u * 8 + w * 2 + cc) if half == 0 else (w * 8 + u * 2 + cc)

    def cols(half):
        return slice(half * 128, half * 128 + 128)

    first = {}
    for off in (2, 1, 3, 0):
        for half in (0, 1):
            u = (coord[axes[half][0]] + off) % 4

            @pl.loop(0, 4)
            def _(w):
                A[half, off, w] = tile_ref[slot_ref[block(half, u, w, 1 - c)], :, cols(half)]
            first[half, off] = send(A.at[half, off], B.at[half, off], s0.at[half * 4 + off], r0.at[half * 4 + off], sib)

    def group(G, base, kind):
        me = {"z": z, "x": x, "y": y}[kind]
        cps = [send(G.at[me], G.at[me], sg.at[base + o], rg.at[base + o], along(kind, o)) for o in (1, 2, 3)]
        return cps

    def gsum(G, cps):
        for cp in cps:
            cp.wait_recv()
        return (G[0] + G[1]) + (G[2] + G[3])

    def own_sum(half, off):
        first[half, off].wait_recv()
        u = (coord[axes[half][0]] + off) % 4

        @pl.loop(0, 4)
        def _(w):
            mine = tile_ref[slot_ref[block(half, u, w, c)], :, cols(half)]
            cur[half, off, w] = (mine.astype(F32) + B[half, off, w].astype(F32)).astype(BF)

    def s1send(k, half, src, dst, off):
        return send(src, dst, s1.at[half, k], r1.at[half, k], along(axes[half][0], off))

    c1 = {}
    for half in (0, 1):
        own_sum(half, 2)
        c1[half, 0] = s1send(0, half, cur.at[half, 2, 0:2], R1.at[half, 0], 1)
        c1[half, 1] = s1send(1, half, cur.at[half, 2, 2:4], R1.at[half, 1], 3)
    for half in (0, 1):
        own_sum(half, 1)
        c1[half, 2] = s1send(2, half, cur.at[half, 1, 2:4], R2.at[half, 0, 2:4], 1)
        own_sum(half, 3)
        c1[half, 3] = s1send(3, half, cur.at[half, 3, 0:2], R2.at[half, 1, 0:2], 3)
    gcp.wait_recv()
    GZ[z] = g_ref[...] + GS[...]
    gz = group(GZ, 0, "z")
    for half in (0, 1):
        own_sum(half, 0)
    for half in (0, 1):
        c1[half, 0].wait_recv()

        @pl.loop(0, 2)
        def _(w):
            cur[half, 1, w] = (cur[half, 1, w].astype(F32) + R1[half, 0, w].astype(F32)).astype(BF)
        c1[half, 4] = s1send(4, half, cur.at[half, 1, 0:2], R2.at[half, 0, 0:2], 1)
        c1[half, 1].wait_recv()

        @pl.loop(0, 2)
        def _(w):
            cur[half, 3, w + 2] = (cur[half, 3, w + 2].astype(F32) + R1[half, 1, w].astype(F32)).astype(BF)
        c1[half, 5] = s1send(5, half, cur.at[half, 3, 2:4], R2.at[half, 1, 2:4], 3)
    GX[x] = gsum(GZ, gz)
    gx = group(GX, 3, "x")

    def s2send(k, half, src, dst, off):
        return send(src, dst, s2.at[half, k], r2.at[half, k], along(axes[half][1], off))

    lo, hi = slice(0, 256), slice(256, 512)
    c2 = {}
    for half in (0, 1):
        for k in (2, 3, 4, 5):
            c1[half, k].wait_recv()
        cw = coord[axes[half][1]]

        @pl.loop(0, 4)
        def _(o):
            w = (cw + o) % 4
            T[half, o] = (cur[half, 0, w].astype(F32) + R2[half, 0, w].astype(F32)
                          + R2[half, 1, w].astype(F32)).astype(BF)
        c2[half, 0] = s2send(0, half, T.at[half, 2, lo], Q1.at[half, 0], 1)
        c2[half, 1] = s2send(1, half, T.at[half, 2, hi], Q1.at[half, 1], 3)
        c2[half, 2] = s2send(2, half, T.at[half, 1, hi], Q2.at[half, 0, hi], 1)
        c2[half, 3] = s2send(3, half, T.at[half, 3, lo], Q2.at[half, 1, lo], 3)
    GY[y] = gsum(GX, gx)
    gy = group(GY, 6, "y")
    for half in (0, 1):
        c2[half, 0].wait_recv()
        T[half, 1, lo] = (T[half, 1, lo].astype(F32) + Q1[half, 0].astype(F32)).astype(BF)
        c2[half, 4] = s2send(4, half, T.at[half, 1, lo], Q2.at[half, 0, lo], 1)
        c2[half, 1].wait_recv()
        T[half, 3, hi] = (T[half, 3, hi].astype(F32) + Q1[half, 1].astype(F32)).astype(BF)
        c2[half, 5] = s2send(5, half, T.at[half, 3, hi], Q2.at[half, 1, hi], 3)
    gout_ref[...] = gsum(GY, gy)
    for half in (0, 1):
        for k in (2, 3, 4, 5):
            c2[half, k].wait_recv()
        out = T[half, 0].astype(F32) + Q2[half, 0].astype(F32) + Q2[half, 1].astype(F32)
        if half == 0:
            dk_ref[...] = out
        else:
            dv_ref[...] = out.astype(BF)
    for cp in pending:
        cp.wait_send()


def scatter(slot, tile, g):
    V = functools.partial(pl.BlockSpec, memory_space=pltpu.VMEM)
    D = pltpu.SemaphoreType.DMA
    return pl.pallas_call(
        scatter_kernel,
        out_shape=(jax.ShapeDtypeStruct((512, 128), F32), jax.ShapeDtypeStruct((512, 128), BF),
                   jax.ShapeDtypeStruct((8, 128), F32)),
        in_specs=[pl.BlockSpec(memory_space=pltpu.SMEM), pl.BlockSpec(memory_space=pl.ANY), V()],
        out_specs=(V(), V(), V()),
        scratch_shapes=[
            pltpu.VMEM((10, 512, 256), BF), D(()),
            pltpu.VMEM((2, 4, 4, 512, 128), BF), pltpu.VMEM((2, 4, 4, 512, 128), BF), pltpu.VMEM((2, 4, 4, 512, 128), BF),
            pltpu.VMEM((2, 2, 2, 512, 128), BF), pltpu.VMEM((2, 2, 4, 512, 128), BF),
            pltpu.VMEM((2, 4, 512, 128), BF), pltpu.VMEM((2, 2, 256, 128), BF), pltpu.VMEM((2, 2, 512, 128), BF),
            pltpu.VMEM((8, 128), F32), pltpu.VMEM((4, 8, 128), F32), pltpu.VMEM((4, 8, 128), F32), pltpu.VMEM((4, 8, 128), F32),
            D((8,)), D((8,)), D((2, 6)), D((2, 6)), D((2, 6)), D((2, 6)), D((10,)), D((10,)),
        ],
        compiler_params=pltpu.CompilerParams(collective_id=1, has_side_effects=True, vmem_limit_bytes=62 * 2 ** 20),
    )(slot, tile, g)


def gather_kernel(k_ref, v_ref, q_ref, do_ref, qg_ref, kg_ref, ko_ref, vo_ref, rows_out, cols_out,
                  kn_ref, q32, do32, rows, cols, lsem, psem, ss, rs):
    z, x, c, y = place()

    def along(axis, off):
        return peer((z + off) % 4, x, c, y) if axis == "z" else peer(z, (x + off) % 4, c, y)

    _, _, kn = norm_fwd(k_ref[...], kg_ref[...])
    kn_ref[...] = kn
    sib = peer(z, x, 1 - c, y)
    greet([sib] + [along(a, o) for a in "zx" for o in (1, 3)])
    coord = {"z": z, "x": x}
    pending = []
    sibling = []
    count = [0, 0]

    halves = ((kn_ref, ko_ref, "x", "z"), (v_ref, vo_ref, "z", "x"))
    lo, hi, full = slice(0, 256), slice(256, 512), slice(0, 512)

    def block(half, uo, wo, cc=None):
        cc = c if cc is None else cc
        u = (coord[halves[half][2]] + uo) % 4
        w = (coord[halves[half][3]] + wo) % 4
        return u * 2 + w * 8 + cc if half == 0 else u * 8 + w * 2 + cc

    def send(half, uo, wo, rows, to, src=None):
        out = halves[half][1]
        k = count[half]
        count[half] += 1
        b = block(half, uo, wo)
        cp = pltpu.make_async_remote_copy(
            src_ref=out.at[b, rows] if src is None else src, dst_ref=out.at[b, rows],
            send_sem=ss.at[half, k], recv_sem=rs.at[half, k], device_id=to, device_id_type=MESH)
        cp.start()
        pending.append(cp)
        return cp

    local = []
    for half, (src, out, u, w) in enumerate(halves):
        cp = pltpu.make_async_copy(src, out.at[block(half, 0, 0)], lsem.at[half])
        cp.start()
        local.append(cp)
    got = {}
    for half, (src, out, u, w) in enumerate(halves):
        got[half, "u+"] = send(half, 0, 0, full, along(u, 1), src)
        got[half, "u-"] = send(half, 0, 0, full, along(u, 3), src)
    q32[...] = q_ref[...].astype(F32)
    do32[...] = do_ref[...].astype(F32)

    def prep(h):
        x = q32[pl.ds(h, 512, stride=8), :]
        _, _, qn = norm_fwd(x, qg_ref[...])
        d = do32[pl.ds(h, 512, stride=8), :].astype(BF)
        rows[h, 0] = x.astype(BF)
        rows[h, 1] = qn
        rows[h, 2] = d
        cols[h, 0] = qn.T
        cols[h, 1] = d.T
        for n, (src, dst) in enumerate(((rows, rows_out), (cols, cols_out))):
            cp = pltpu.make_async_copy(src.at[h], dst.at[h], psem.at[n, h])
            cp.start()
            local.append(cp)

    for half, (src, out, u, w) in enumerate(halves):
        got[half, 0, "w+"] = send(half, 0, 0, full, along(w, 1), src)
        got[half, 0, "w-"] = send(half, 0, 0, full, along(w, 3), src)
        sibling.append(send(half, 0, 0, full, sib, src))
    prep(0)
    for half, (src, out, u, w) in enumerate(halves):
        got[half, "u+"].wait_recv()
        got[half, "f+"] = send(half, 3, 0, lo, along(u, 1))
        got[half, 3, "w+"] = send(half, 3, 0, full, along(w, 1))
        got[half, 3, "w-"] = send(half, 3, 0, full, along(w, 3))
        sibling.append(send(half, 3, 0, full, sib))
        got[half, "u-"].wait_recv()
        got[half, "f-"] = send(half, 1, 0, hi, along(u, 3))
        got[half, 1, "w+"] = send(half, 1, 0, full, along(w, 1))
        got[half, 1, "w-"] = send(half, 1, 0, full, along(w, 3))
        sibling.append(send(half, 1, 0, full, sib))

    def onward(half, uo):
        w = halves[half][3]
        got[half, uo, "w+"].wait_recv()
        got[half, uo, "g+"] = send(half, uo, 3, lo, along(w, 1))
        sibling.append(send(half, uo, 3, full, sib))
        got[half, uo, "w-"].wait_recv()
        got[half, uo, "g-"] = send(half, uo, 1, hi, along(w, 3))
        sibling.append(send(half, uo, 1, full, sib))

    prep(1)
    for half in (0, 1):
        onward(half, 0)
    prep(2)
    for half, (src, out, u, w) in enumerate(halves):
        got[half, "f+"].wait_recv()
        got[half, "f-"].wait_recv()
        got[half, 2, "w+"] = send(half, 2, 0, full, along(w, 1))
        got[half, 2, "w-"] = send(half, 2, 0, full, along(w, 3))
        sibling.append(send(half, 2, 0, full, sib))
    for uo in (3, 1, 2):
        prep(3 + (uo % 3))
        for half in (0, 1):
            onward(half, uo)
    prep(6)
    prep(7)
    for uo in (0, 3, 1, 2):
        for half in (0, 1):
            got[half, uo, "g+"].wait_recv()
            got[half, uo, "g-"].wait_recv()
            sibling.append(send(half, uo, 2, full, sib))
    for cp in sibling:
        cp.wait_recv()
    for cp in pending:
        cp.wait_send()
    for cp in local:
        cp.wait()


def gather(k, v, q, do, qg, kg):
    D = pltpu.SemaphoreType.DMA
    anys = pl.BlockSpec(memory_space=pl.ANY)
    vm = pl.BlockSpec(memory_space=pltpu.VMEM)
    return pl.pallas_call(
        gather_kernel,
        out_shape=(jax.ShapeDtypeStruct((32, 512, 128), BF), jax.ShapeDtypeStruct((32, 512, 128), BF),
                   jax.ShapeDtypeStruct((8, 3, 512, 128), BF), jax.ShapeDtypeStruct((8, 2, 128, 512), BF)),
        in_specs=[vm] * 6,
        out_specs=(anys,) * 4,
        scratch_shapes=[
            pltpu.VMEM((512, 128), BF), pltpu.VMEM((4096, 128), F32), pltpu.VMEM((4096, 128), F32),
            pltpu.VMEM((8, 3, 512, 128), BF), pltpu.VMEM((8, 2, 128, 512), BF),
            D((2,)), D((2, 8)), D((2, 36)), D((2, 36)),
        ],
        compiler_params=pltpu.CompilerParams(collective_id=0, has_side_effects=True, vmem_limit_bytes=60 * 2 ** 20),
    )(k, v, q, do, qg, kg)


def attn(idx, kn_all, v_all, rows, cols, qg, kg):
    H = rows.shape[0]
    V = functools.partial(pl.BlockSpec, memory_space=pltpu.VMEM)
    A = functools.partial(pl.BlockSpec, memory_space=pl.ANY)
    return pl.pallas_call(
        attn_kernel,
        out_shape=(
            jax.ShapeDtypeStruct((512 * H, 128), BF),
            jax.ShapeDtypeStruct((10, 512, 256), BF),
            jax.ShapeDtypeStruct((8, 128), F32),
            jax.ShapeDtypeStruct((40,), jnp.int32),
        ),
        in_specs=[pl.BlockSpec(memory_space=pltpu.SMEM), A(), A(), A(), A(), V(), V()],
        out_specs=(V(), A(), V(), pl.BlockSpec(memory_space=pltpu.SMEM)),
        scratch_shapes=[
            pltpu.VMEM((10, 512, 256), BF),
            pltpu.VMEM((H, 3, 512, 128), BF), pltpu.VMEM((H, 2, 128, 512), BF),
            pltpu.VMEM((8, 128), F32), pltpu.VMEM((8, 128), F32),
            pltpu.VMEM((9, 512, 128), BF), pltpu.VMEM((9, 512, 128), BF),
            pltpu.VMEM((9, 128, 512), BF),
            pltpu.VMEM((9, 512, 512), F32), pltpu.VMEM((9, 512, 512), F32), pltpu.VMEM((9, 512, 512), BF),
            pltpu.VMEM((9, 512, 128), F32), pltpu.VMEM((9, 512, 128), F32),
            pltpu.VMEM((128, 512), F32),
            pltpu.VMEM((2, 8, 512), F32), pltpu.VMEM((4, 8, 512), F32),
            pltpu.VMEM((2, 512, 128), BF), pltpu.VMEM((2, 512, 128), BF),
            pltpu.VMEM((512 * H, 128), F32),
            pltpu.SemaphoreType.DMA((3, 10)), pltpu.SemaphoreType.DMA((2, H)),
        ],
        compiler_params=pltpu.CompilerParams(vmem_limit_bytes=60 * 2 ** 20),
    )(idx, kn_all, v_all, rows, cols, qg, kg)


def on_device(q_raw, k_raw, values, dout, q_gain, k_gain, chosen):
    blk, heads, width = q_raw.shape
    k2, v2 = k_raw.reshape(blk, width), values.reshape(blk, width)
    qg, kg = q_gain[None], k_gain[None]
    kn_all, v_all, rows, cols = gather(
        k2, v2, q_raw.reshape(blk * heads, width), dout.reshape(blk * heads, width), qg, kg)
    dq_raw, tile, parts, slot = attn(chosen.reshape(-1), kn_all, v_all, rows, cols, qg, kg)
    dkn, dvalues, sums = scatter(slot, tile, parts)
    xk, rk, _ = norm_fwd(k2, k_gain)
    dk_raw, _ = norm_back(xk, rk, k_gain, dkn)
    return (
        dq_raw.reshape(blk, heads, width),
        dk_raw.astype(BF).reshape(blk, 1, width),
        dvalues.reshape(blk, 1, width),
        sums[0],
        sums[1],
    )


def solution(mesh):
    tok = P("ctx", "head", None)
    return jax.shard_map(
        on_device,
        mesh=mesh,
        in_specs=(tok, tok, tok, tok, P(), P(), tok),
        out_specs=(tok, tok, tok, P(), P()),
        check_vma=False,
    )
```

```python
import functools

import jax, jax.numpy as jnp
from jax import lax
from jax.experimental import pallas as pl
from jax.experimental.pallas import tpu as pltpu
from jax.sharding import PartitionSpec as P

SC = 128 ** -0.5
C2 = SC * 1.4426950408889634
NEG = -1e30
F32 = jnp.float32
BF = jnp.bfloat16

EPS = 1e-06


def norm_fwd(raw, gain):
    x = raw.astype(jnp.float32)
    scale_r = lax.rsqrt(jnp.mean(x * x, axis=-1, keepdims=True) + EPS)
    return (x, scale_r, (x * scale_r * gain).astype(jnp.bfloat16))


def norm_back(x, scale_r, gain, grad_y):
    along = gain * grad_y
    inner = jnp.mean(along * x, axis=-1, keepdims=True)
    grad_x = scale_r * (along - x * scale_r * scale_r * inner)
    return (grad_x, grad_y * x * scale_r)


def dot(a, b):
    return lax.dot_general(a, b, (((1,), (0,)), ((), ())), preferred_element_type=F32)

def fold(x, op):
    return op(x.reshape(x.shape[0] // 8, 8, x.shape[1]), axis=0)

def attn_kernel(idx_ref, kn_hbm, v_hbm, rows_hbm, cols_hbm, qgain_ref, kgain_ref,
                dq_ref, tile_hbm, g_ref, slot_ref, tile_ref, rows_ref, cols_ref, kg_ref, gq_ref,
                kb, vb, kT, S, DP, E, dk, dv, dqT, mrow, drow, qs, dos, dq32, sem, hsem):
    H = rows_hbm.shape[0]
    J = 9
    me = lax.axis_index("ctx")
    def operand(j, own, n):
        blk = me if own else jnp.maximum(idx_ref[j], 0)
        src, dst = ((kn_hbm, kb), (v_hbm, vb))[n]
        return pltpu.make_async_copy(src.at[blk], dst.at[j], sem.at[n, j])

    def tile_out(j):
        return pltpu.make_async_copy(tile_ref.at[j], tile_hbm.at[j], sem.at[2, j])

    def operands(h):
        return (pltpu.make_async_copy(rows_hbm.at[h], rows_ref.at[h], hsem.at[0, h]),
                pltpu.make_async_copy(cols_hbm.at[h], cols_ref.at[h], hsem.at[1, h]))

    for cp in operands(0):
        cp.start()
    for n in (0, 1):
        for j in range(J):
            operand(j, j == J - 1, n).start()
    for h in range(1, H):
        for cp in operands(h):
            cp.start()
    for b in range(40):
        slot_ref[b] = J
    for j in range(J - 1):
        slot_ref[jnp.where(idx_ref[j] >= 0, idx_ref[j], 32)] = j
    slot_ref[me] = J - 1
    kg_ref[...] = jnp.zeros(kg_ref.shape, F32)
    gq_ref[...] = jnp.zeros(gq_ref.shape, F32)
    tile_ref[J] = jnp.zeros(tile_ref.shape[1:], BF)
    tile_out(J).start()

    rows = lax.broadcasted_iota(jnp.int32, (512, 512), 0)
    cols = lax.broadcasted_iota(jnp.int32, (512, 512), 1)

    def A1(h, j, own):
        s = dot(kb[j], cols_ref[h, 0])
        if own:
            s = jnp.where(rows <= cols, s, NEG)
        S[j] = s
        cm = fold(s, jnp.max)
        if not own:
            cm = jnp.where(idx_ref[j] >= 0, cm, NEG)
        return cm

    def A2(h, j, own):
        m = mrow[h % 2]
        if not own:
            m = jnp.where(idx_ref[j] >= 0, m, 1e30)
        s = S[j]
        e = jnp.exp2((s.reshape(64, 8, 512) - m[None]) * C2)
        l = jnp.sum(e, axis=0)
        eb = e.reshape(512, 512).astype(BF)
        E[j] = eb
        dp = dot(vb[j], cols_ref[h, 1])
        DP[j] = dp
        return l, fold(e.reshape(512, 512) * dp, jnp.sum)

    def C(h, j):
        dp = DP[j]
        dl = drow[h % 2]
        dpb = (dp.reshape(64, 8, 512) - dl[None]).reshape(512, 512).astype(BF)
        eb = E[j]
        ds = eb * dpb
        dv[j] += dot(eb, dos[h % 2])
        dk[j] += dot(ds, qs[h % 2])
        dqT[...] += dot(kT[j], ds)

    def step(t, a1, a2, c):
        if a1:
            for cp in operands(t):
                cp.wait()
        if c:
            dqT[...] = jnp.zeros(dqT.shape, F32)

        def body(j, carry, own=False):
            mx, l, dd = carry
            if a1 and not a2:
                operand(j, own, 0).wait()
            if a1 and a2 and not c:
                operand(j, own, 1).wait()
                kT[j] = kb[j].T
                dk[j] = jnp.zeros(dk.shape[1:], F32)
                dv[j] = jnp.zeros(dv.shape[1:], F32)
            if c:
                C(t - 2, j)
            if a2:
                l_j, d_j = A2(t - 1, j, own)
                l, dd = l + l_j, dd + d_j
            if a1:
                mx = jnp.maximum(mx, A1(t, j, own))
            if c and not a2:
                kg_ref[...] += fold(dk[j] * kb[j].astype(F32), jnp.sum)
                tile_ref[j, :, 0:128] = dk[j].astype(BF)
                tile_ref[j, :, 128:256] = dv[j].astype(BF)
                tile_out(j).start()
            return mx, l, dd
        carry = (jnp.full((8, 512), NEG, F32), jnp.zeros((8, 512), F32), jnp.zeros((8, 512), F32))
        carry = lax.fori_loop(0, J - 1, body, carry, unroll=8)
        mx, l, dd = body(J - 1, carry, True)
        if c:
            h = t - 2
            rl = drow[h % 2 + 2]
            dq = (dqT[...] * (rl[:1] * SC)).T
            x = rows_ref[h, 0].astype(F32)
            rq = lax.rsqrt(jnp.mean(x * x, axis=1, keepdims=True) + EPS)
            dq_raw, gq = norm_back(x, rq, qgain_ref[...], dq)
            dq32[pl.ds(h, 512, stride=8), :] = dq_raw
            gq_ref[...] += fold(gq, jnp.sum)
        if a2:
            h = t - 1
            l1 = jnp.sum(l, axis=0, keepdims=True)
            rl = jnp.broadcast_to(1.0 / l1, (8, 512))
            dl = jnp.sum(dd, axis=0, keepdims=True) * rl[:1]
            drow[h % 2] = jnp.broadcast_to(dl, (8, 512))
            drow[h % 2 + 2] = rl
            rc = rl.T[:, :1]
            dos[h % 2] = (rows_ref[h, 2].astype(F32) * rc).astype(BF)
            qs[h % 2] = (rows_ref[h, 1].astype(F32) * (rc * SC)).astype(BF)
        if a1:
            m = jnp.max(mx, axis=0, keepdims=True)
            mrow[t % 2] = jnp.broadcast_to(m, (8, 512))

    step(0, True, False, False)
    step(1, True, True, False)

    @pl.loop(2, H)
    def _(t):
        step(t, True, True, True)
    step(H, False, True, True)
    step(H + 1, False, False, True)

    dq_ref[...] = dq32[...].astype(BF)
    part_q = jnp.sum(gq_ref[...], axis=0, keepdims=True)
    part_k = jnp.sum(kg_ref[...], axis=0, keepdims=True) / kgain_ref[...]
    row = lax.broadcasted_iota(jnp.int32, (8, 128), 0)
    g_ref[...] = jnp.where(row == 0, part_q, jnp.where(row == 1, part_k, 0.0))
    for j in range(J + 1):
        tile_out(j).wait()


MESH = pl.DeviceIdType.MESH


def place():
    ctx, y = lax.axis_index("ctx"), lax.axis_index("head")
    return ctx // 8, (ctx // 2) % 4, ctx % 2, y


def peer(z, x, c, y):
    return (z * 8 + x * 2 + c, y)


def hail(devices):
    for d in devices:
        pl.semaphore_signal(pltpu.get_barrier_semaphore(), inc=1, device_id=d, device_id_type=MESH)


def settle(devices):
    pl.semaphore_wait(pltpu.get_barrier_semaphore(), len(devices))


def scatter_kernel(slot_ref, tile_hbm, g_ref, dk_ref, dv_ref, gout_ref,
                   tile_ref, tsem, A, B, cur, R1, R2, T, Q1, Q2, GS, GZ, GX, GY,
                   s0, r0, s1, r1, s2, r2, sg, rg):
    z, x, c, y = place()

    def along(axis, off):
        if axis == "z":
            return peer((z + off) % 4, x, c, y)
        if axis == "x":
            return peer(z, (x + off) % 4, c, y)
        return peer(z, x, c, (y + off) % 4)

    fetch = pltpu.make_async_copy(tile_hbm.at[0:10], tile_ref, tsem)
    fetch.start()
    sib = peer(z, x, 1 - c, y)
    friends = [sib] + [along(a, o) for a in "zxy" for o in (1, 2, 3)]
    hail(friends)
    pending = []

    def send(src, dst, ss, rs, to):
        cp = pltpu.make_async_remote_copy(src_ref=src, dst_ref=dst, send_sem=ss, recv_sem=rs,
                                          device_id=to, device_id_type=MESH)
        cp.start()
        pending.append(cp)
        return cp

    axes = (("z", "x"), ("x", "z"))
    coord = {"z": z, "x": x}

    def block(half, u, w, cc):
        return (u * 8 + w * 2 + cc) if half == 0 else (w * 8 + u * 2 + cc)

    def cols(half):
        return slice(half * 128, half * 128 + 128)

    first = {}

    def fill(half, off):
        u = (coord[axes[half][0]] + off) % 4

        @pl.loop(0, 4)
        def _(w):
            A[half, off, w] = tile_ref[slot_ref[block(half, u, w, 1 - c)], :, cols(half)]

    fetch.wait()
    fill(0, 2)
    fill(1, 2)
    settle(friends)
    gcp = send(g_ref, GS, sg.at[0], rg.at[0], sib)
    for off in (2, 1, 3, 0):
        for half in (0, 1):
            if off != 2:
                fill(half, off)
            first[half, off] = send(A.at[half, off], B.at[half, off], s0.at[half * 4 + off], r0.at[half * 4 + off], sib)

    def group(G, base, kind):
        me = {"z": z, "x": x, "y": y}[kind]
        cps = [send(G.at[me], G.at[me], sg.at[base + o], rg.at[base + o], along(kind, o)) for o in (1, 2, 3)]
        return cps

    def gsum(G, cps):
        for cp in cps:
            cp.wait_recv()
        return (G[0] + G[1]) + (G[2] + G[3])

    def own_sum(half, off):
        first[half, off].wait_recv()
        u = (coord[axes[half][0]] + off) % 4

        @pl.loop(0, 4)
        def _(w):
            mine = tile_ref[slot_ref[block(half, u, w, c)], :, cols(half)]
            cur[half, off, w] = (mine.astype(F32) + B[half, off, w].astype(F32)).astype(BF)

    def s1send(k, half, src, dst, off):
        return send(src, dst, s1.at[half, k], r1.at[half, k], along(axes[half][0], off))

    c1 = {}
    for half in (0, 1):
        own_sum(half, 2)
        c1[half, 0] = s1send(0, half, cur.at[half, 2, 0:2], R1.at[half, 0], 1)
        c1[half, 1] = s1send(1, half, cur.at[half, 2, 2:4], R1.at[half, 1], 3)
    for half in (0, 1):
        own_sum(half, 1)
        c1[half, 2] = s1send(2, half, cur.at[half, 1, 2:4], R2.at[half, 0, 2:4], 1)
        own_sum(half, 3)
        c1[half, 3] = s1send(3, half, cur.at[half, 3, 0:2], R2.at[half, 1, 0:2], 3)
    gcp.wait_recv()
    GZ[z] = g_ref[...] + GS[...]
    gz = group(GZ, 0, "z")
    for half in (0, 1):
        own_sum(half, 0)
    for half in (0, 1):
        c1[half, 0].wait_recv()

        @pl.loop(0, 2)
        def _(w):
            cur[half, 1, w] = (cur[half, 1, w].astype(F32) + R1[half, 0, w].astype(F32)).astype(BF)
        c1[half, 4] = s1send(4, half, cur.at[half, 1, 0:2], R2.at[half, 0, 0:2], 1)
        c1[half, 1].wait_recv()

        @pl.loop(0, 2)
        def _(w):
            cur[half, 3, w + 2] = (cur[half, 3, w + 2].astype(F32) + R1[half, 1, w].astype(F32)).astype(BF)
        c1[half, 5] = s1send(5, half, cur.at[half, 3, 2:4], R2.at[half, 1, 2:4], 3)
    GX[x] = gsum(GZ, gz)
    gx = group(GX, 3, "x")

    def s2send(k, half, src, dst, off):
        return send(src, dst, s2.at[half, k], r2.at[half, k], along(axes[half][1], off))

    lo, hi = slice(0, 256), slice(256, 512)
    c2 = {}
    for half in (0, 1):
        for k in (2, 3, 4, 5):
            c1[half, k].wait_recv()
        cw = coord[axes[half][1]]

        @pl.loop(0, 4)
        def _(o):
            w = (cw + o) % 4
            T[half, o] = (cur[half, 0, w].astype(F32) + R2[half, 0, w].astype(F32)
                          + R2[half, 1, w].astype(F32)).astype(BF)
        c2[half, 0] = s2send(0, half, T.at[half, 2, lo], Q1.at[half, 0], 1)
        c2[half, 1] = s2send(1, half, T.at[half, 2, hi], Q1.at[half, 1], 3)
        c2[half, 2] = s2send(2, half, T.at[half, 1, hi], Q2.at[half, 0, hi], 1)
        c2[half, 3] = s2send(3, half, T.at[half, 3, lo], Q2.at[half, 1, lo], 3)
    GY[y] = gsum(GX, gx)
    gy = group(GY, 6, "y")
    for half in (0, 1):
        c2[half, 0].wait_recv()
        T[half, 1, lo] = (T[half, 1, lo].astype(F32) + Q1[half, 0].astype(F32)).astype(BF)
        c2[half, 4] = s2send(4, half, T.at[half, 1, lo], Q2.at[half, 0, lo], 1)
        c2[half, 1].wait_recv()
        T[half, 3, hi] = (T[half, 3, hi].astype(F32) + Q1[half, 1].astype(F32)).astype(BF)
        c2[half, 5] = s2send(5, half, T.at[half, 3, hi], Q2.at[half, 1, hi], 3)
    gout_ref[...] = gsum(GY, gy)
    for half in (0, 1):
        for k in (2, 3, 4, 5):
            c2[half, k].wait_recv()
        out = T[half, 0].astype(F32) + Q2[half, 0].astype(F32) + Q2[half, 1].astype(F32)
        if half == 0:
            dk_ref[...] = out
        else:
            dv_ref[...] = out.astype(BF)
    for cp in pending:
        cp.wait_send()


def scatter(slot, tile, g):
    V = functools.partial(pl.BlockSpec, memory_space=pltpu.VMEM)
    D = pltpu.SemaphoreType.DMA
    return pl.pallas_call(
        scatter_kernel,
        out_shape=(jax.ShapeDtypeStruct((512, 128), F32), jax.ShapeDtypeStruct((512, 128), BF),
                   jax.ShapeDtypeStruct((8, 128), F32)),
        in_specs=[pl.BlockSpec(memory_space=pltpu.SMEM), pl.BlockSpec(memory_space=pl.ANY), V()],
        out_specs=(V(), V(), V()),
        scratch_shapes=[
            pltpu.VMEM((10, 512, 256), BF), D(()),
            pltpu.VMEM((2, 4, 4, 512, 128), BF), pltpu.VMEM((2, 4, 4, 512, 128), BF), pltpu.VMEM((2, 4, 4, 512, 128), BF),
            pltpu.VMEM((2, 2, 2, 512, 128), BF), pltpu.VMEM((2, 2, 4, 512, 128), BF),
            pltpu.VMEM((2, 4, 512, 128), BF), pltpu.VMEM((2, 2, 256, 128), BF), pltpu.VMEM((2, 2, 512, 128), BF),
            pltpu.VMEM((8, 128), F32), pltpu.VMEM((4, 8, 128), F32), pltpu.VMEM((4, 8, 128), F32), pltpu.VMEM((4, 8, 128), F32),
            D((8,)), D((8,)), D((2, 6)), D((2, 6)), D((2, 6)), D((2, 6)), D((10,)), D((10,)),
        ],
        compiler_params=pltpu.CompilerParams(collective_id=1, has_side_effects=True, vmem_limit_bytes=52 * 2 ** 20),
    )(slot, tile, g)


def gather_kernel(k_ref, v_ref, q_hbm, do_hbm, qg_ref, kg_ref, ko_ref, vo_ref, rows_out, cols_out,
                  kn_ref, qb, db, q32, do32, isem, rows, cols, lsem, psem, ss, rs):
    z, x, c, y = place()

    def along(axis, off):
        return peer((z + off) % 4, x, c, y) if axis == "z" else peer(z, (x + off) % 4, c, y)

    sib = peer(z, x, 1 - c, y)
    friends = [sib] + [along(a, o) for a in "zx" for o in (1, 3)]
    hail(friends)
    loads = [pltpu.make_async_copy(q_hbm, qb, isem.at[0]), pltpu.make_async_copy(do_hbm, db, isem.at[1])]
    for cp in loads:
        cp.start()
    _, _, kn = norm_fwd(k_ref[...], kg_ref[...])
    kn_ref[...] = kn
    settle(friends)
    coord = {"z": z, "x": x}
    pending = []
    sibling = []
    count = [0, 0]

    halves = ((kn_ref, ko_ref, "x", "z"), (v_ref, vo_ref, "z", "x"))
    lo, hi, full = slice(0, 256), slice(256, 512), slice(0, 512)

    def block(half, uo, wo, cc=None):
        cc = c if cc is None else cc
        u = (coord[halves[half][2]] + uo) % 4
        w = (coord[halves[half][3]] + wo) % 4
        return u * 2 + w * 8 + cc if half == 0 else u * 8 + w * 2 + cc

    def send(half, uo, wo, rows, to, src=None):
        out = halves[half][1]
        k = count[half]
        count[half] += 1
        b = block(half, uo, wo)
        cp = pltpu.make_async_remote_copy(
            src_ref=out.at[b, rows] if src is None else src, dst_ref=out.at[b, rows],
            send_sem=ss.at[half, k], recv_sem=rs.at[half, k], device_id=to, device_id_type=MESH)
        cp.start()
        pending.append(cp)
        return cp

    local = []
    for half, (src, out, u, w) in enumerate(halves):
        cp = pltpu.make_async_copy(src, out.at[block(half, 0, 0)], lsem.at[half])
        cp.start()
        local.append(cp)
    got = {}
    for half, (src, out, u, w) in enumerate(halves):
        got[half, "u+"] = send(half, 0, 0, full, along(u, 1), src)
        got[half, "u-"] = send(half, 0, 0, full, along(u, 3), src)
    def prep(h):
        x = q32[pl.ds(h, 512, stride=8), :]
        _, _, qn = norm_fwd(x, qg_ref[...])
        d = do32[pl.ds(h, 512, stride=8), :].astype(BF)
        rows[h, 0] = x.astype(BF)
        rows[h, 1] = qn
        rows[h, 2] = d
        cols[h, 0] = qn.T
        cols[h, 1] = d.T
        for n, (src, dst) in enumerate(((rows, rows_out), (cols, cols_out))):
            cp = pltpu.make_async_copy(src.at[h], dst.at[h], psem.at[n, h])
            cp.start()
            local.append(cp)

    for half, (src, out, u, w) in enumerate(halves):
        got[half, 0, "w+"] = send(half, 0, 0, full, along(w, 1), src)
        got[half, 0, "w-"] = send(half, 0, 0, full, along(w, 3), src)
        sibling.append(send(half, 0, 0, full, sib, src))
    for cp in loads:
        cp.wait()
    q32[...] = qb[...].astype(F32)
    do32[...] = db[...].astype(F32)
    prep(0)
    for half, (src, out, u, w) in enumerate(halves):
        got[half, "u+"].wait_recv()
        got[half, "f+"] = send(half, 3, 0, lo, along(u, 1))
        got[half, 3, "w+"] = send(half, 3, 0, full, along(w, 1))
        got[half, 3, "w-"] = send(half, 3, 0, full, along(w, 3))
        sibling.append(send(half, 3, 0, full, sib))
        got[half, "u-"].wait_recv()
        got[half, "f-"] = send(half, 1, 0, hi, along(u, 3))
        got[half, 1, "w+"] = send(half, 1, 0, full, along(w, 1))
        got[half, 1, "w-"] = send(half, 1, 0, full, along(w, 3))
        sibling.append(send(half, 1, 0, full, sib))

    def onward(half, uo):
        w = halves[half][3]
        got[half, uo, "w+"].wait_recv()
        got[half, uo, "g+"] = send(half, uo, 3, lo, along(w, 1))
        sibling.append(send(half, uo, 3, full, sib))
        got[half, uo, "w-"].wait_recv()
        got[half, uo, "g-"] = send(half, uo, 1, hi, along(w, 3))
        sibling.append(send(half, uo, 1, full, sib))

    prep(1)
    for half in (0, 1):
        onward(half, 0)
    prep(2)
    for half, (src, out, u, w) in enumerate(halves):
        got[half, "f+"].wait_recv()
        got[half, "f-"].wait_recv()
        got[half, 2, "w+"] = send(half, 2, 0, full, along(w, 1))
        got[half, 2, "w-"] = send(half, 2, 0, full, along(w, 3))
        sibling.append(send(half, 2, 0, full, sib))
    for uo in (3, 1, 2):
        prep(3 + (uo % 3))
        for half in (0, 1):
            onward(half, uo)
    prep(6)
    prep(7)
    for uo in (0, 3, 1, 2):
        for half in (0, 1):
            got[half, uo, "g+"].wait_recv()
            got[half, uo, "g-"].wait_recv()
            sibling.append(send(half, uo, 2, full, sib))
    for cp in sibling:
        cp.wait_recv()
    for cp in pending:
        cp.wait_send()
    for cp in local:
        cp.wait()


def gather(k, v, q, do, qg, kg):
    D = pltpu.SemaphoreType.DMA
    anys = pl.BlockSpec(memory_space=pl.ANY)
    vm = pl.BlockSpec(memory_space=pltpu.VMEM)
    return pl.pallas_call(
        gather_kernel,
        out_shape=(jax.ShapeDtypeStruct((32, 512, 128), BF), jax.ShapeDtypeStruct((32, 512, 128), BF),
                   jax.ShapeDtypeStruct((8, 3, 512, 128), BF), jax.ShapeDtypeStruct((8, 2, 128, 512), BF)),
        in_specs=[vm, vm, anys, anys, vm, vm],
        out_specs=(anys,) * 4,
        scratch_shapes=[
            pltpu.VMEM((512, 128), BF), pltpu.VMEM((4096, 128), BF), pltpu.VMEM((4096, 128), BF),
            pltpu.VMEM((4096, 128), F32), pltpu.VMEM((4096, 128), F32), D((2,)),
            pltpu.VMEM((8, 3, 512, 128), BF), pltpu.VMEM((8, 2, 128, 512), BF),
            D((2,)), D((2, 8)), D((2, 36)), D((2, 36)),
        ],
        compiler_params=pltpu.CompilerParams(collective_id=0, has_side_effects=True, vmem_limit_bytes=60 * 2 ** 20),
    )(k, v, q, do, qg, kg)


def attn(idx, kn_all, v_all, rows, cols, qg, kg):
    H = rows.shape[0]
    V = functools.partial(pl.BlockSpec, memory_space=pltpu.VMEM)
    A = functools.partial(pl.BlockSpec, memory_space=pl.ANY)
    return pl.pallas_call(
        attn_kernel,
        out_shape=(
            jax.ShapeDtypeStruct((512 * H, 128), BF),
            jax.ShapeDtypeStruct((64, 512, 256), BF),
            jax.ShapeDtypeStruct((8, 128), F32),
            jax.ShapeDtypeStruct((40,), jnp.int32),
        ),
        in_specs=[pl.BlockSpec(memory_space=pltpu.SMEM), A(), A(), A(), A(), V(), V()],
        out_specs=(V(), A(), V(), pl.BlockSpec(memory_space=pltpu.SMEM)),
        scratch_shapes=[
            pltpu.VMEM((10, 512, 256), BF),
            pltpu.VMEM((H, 3, 512, 128), BF), pltpu.VMEM((H, 2, 128, 512), BF),
            pltpu.VMEM((8, 128), F32), pltpu.VMEM((8, 128), F32),
            pltpu.VMEM((9, 512, 128), BF), pltpu.VMEM((9, 512, 128), BF),
            pltpu.VMEM((9, 128, 512), BF),
            pltpu.VMEM((9, 512, 512), F32), pltpu.VMEM((9, 512, 512), F32), pltpu.VMEM((9, 512, 512), BF),
            pltpu.VMEM((9, 512, 128), F32), pltpu.VMEM((9, 512, 128), F32),
            pltpu.VMEM((128, 512), F32),
            pltpu.VMEM((2, 8, 512), F32), pltpu.VMEM((4, 8, 512), F32),
            pltpu.VMEM((2, 512, 128), BF), pltpu.VMEM((2, 512, 128), BF),
            pltpu.VMEM((512 * H, 128), F32),
            pltpu.SemaphoreType.DMA((3, 10)), pltpu.SemaphoreType.DMA((2, H)),
        ],
        compiler_params=pltpu.CompilerParams(vmem_limit_bytes=60 * 2 ** 20),
    )(idx, kn_all, v_all, rows, cols, qg, kg)


def on_device(q_raw, k_raw, values, dout, q_gain, k_gain, chosen):
    blk, heads, width = q_raw.shape
    k2, v2 = k_raw.reshape(blk, width), values.reshape(blk, width)
    qg, kg = q_gain[None], k_gain[None]
    kn_all, v_all, rows, cols = gather(
        k2, v2, q_raw.reshape(blk * heads, width), dout.reshape(blk * heads, width), qg, kg)
    dq_raw, tile, parts, slot = attn(chosen.reshape(-1), kn_all, v_all, rows, cols, qg, kg)
    dkn, dvalues, sums = scatter(slot, tile, parts)
    xk, rk, _ = norm_fwd(k2, k_gain)
    dk_raw, _ = norm_back(xk, rk, k_gain, dkn)
    return (
        dq_raw.reshape(blk, heads, width),
        dk_raw.astype(BF).reshape(blk, 1, width),
        dvalues.reshape(blk, 1, width),
        sums[0],
        sums[1],
    )


def solution(mesh):
    tok = P("ctx", "head", None)
    return jax.shard_map(
        on_device,
        mesh=mesh,
        in_specs=(tok, tok, tok, tok, P(), P(), tok),
        out_specs=(tok, tok, tok, P(), P()),
        check_vma=False,
    )
```

```python
import functools

import jax, jax.numpy as jnp
from jax import lax
from jax.experimental import pallas as pl
from jax.experimental.pallas import tpu as pltpu
from jax.sharding import PartitionSpec as P

SC = 128 ** -0.5
C2 = SC * 1.4426950408889634
NEG = -1e30
F32 = jnp.float32
BF = jnp.bfloat16

EPS = 1e-06


def norm_fwd(raw, gain):
    x = raw.astype(jnp.float32)
    scale_r = lax.rsqrt(jnp.mean(x * x, axis=-1, keepdims=True) + EPS)
    return (x, scale_r, (x * scale_r * gain).astype(jnp.bfloat16))


def norm_back(x, scale_r, gain, grad_y):
    along = gain * grad_y
    inner = jnp.mean(along * x, axis=-1, keepdims=True)
    grad_x = scale_r * (along - x * scale_r * scale_r * inner)
    return (grad_x, grad_y * x * scale_r)


def dot(a, b):
    return lax.dot_general(a, b, (((1,), (0,)), ((), ())), preferred_element_type=F32)

def fold(x, op):
    return op(x.reshape(x.shape[0] // 8, 8, x.shape[1]), axis=0)

def attn_kernel(idx_ref, kn_hbm, v_hbm, rows_hbm, cols_hbm, qgain_ref, kgain_ref,
                dq_ref, tile_hbm, g_hbm, slot_ref, tile_ref, g_ref, rows_ref, cols_ref, kg_ref, gq_ref,
                kb, vb, kT, S, DP, E, dk, dv, dqT, mrow, drow, qs, dos, dq32, sem, hsem):
    H = rows_hbm.shape[0]
    J = 9
    me = lax.axis_index("ctx")
    def operand(j, own, n):
        blk = me if own else jnp.maximum(idx_ref[j], 0)
        src, dst = ((kn_hbm, kb), (v_hbm, vb))[n]
        return pltpu.make_async_copy(src.at[blk], dst.at[j], sem.at[n, j])

    def tile_out(j):
        return pltpu.make_async_copy(tile_ref.at[j], tile_hbm.at[j], sem.at[2, j])

    def operands(h):
        return (pltpu.make_async_copy(rows_hbm.at[h], rows_ref.at[h], hsem.at[0, h]),
                pltpu.make_async_copy(cols_hbm.at[h], cols_ref.at[h], hsem.at[1, h]))

    for cp in operands(0):
        cp.start()
    for n in (0, 1):
        for j in range(J):
            operand(j, j == J - 1, n).start()
    for h in range(1, H):
        for cp in operands(h):
            cp.start()
    for b in range(40):
        slot_ref[b] = J
    for j in range(J - 1):
        slot_ref[jnp.where(idx_ref[j] >= 0, idx_ref[j], 32)] = j
    slot_ref[me] = J - 1
    kg_ref[...] = jnp.zeros(kg_ref.shape, F32)
    gq_ref[...] = jnp.zeros(gq_ref.shape, F32)
    tile_ref[J] = jnp.zeros(tile_ref.shape[1:], BF)
    tile_out(J).start()

    rows = lax.broadcasted_iota(jnp.int32, (512, 512), 0)
    cols = lax.broadcasted_iota(jnp.int32, (512, 512), 1)

    def A1(h, j, own):
        s = dot(kb[j], cols_ref[h, 0])
        if own:
            s = jnp.where(rows <= cols, s, NEG)
        S[j] = s
        cm = fold(s, jnp.max)
        if not own:
            cm = jnp.where(idx_ref[j] >= 0, cm, NEG)
        return cm

    def A2(h, j, own):
        m = mrow[h % 2]
        if not own:
            m = jnp.where(idx_ref[j] >= 0, m, 1e30)
        s = S[j]
        e = jnp.exp2((s.reshape(64, 8, 512) - m[None]) * C2)
        l = jnp.sum(e, axis=0)
        eb = e.reshape(512, 512).astype(BF)
        E[j] = eb
        dp = dot(vb[j], cols_ref[h, 1])
        DP[j] = dp
        return l, fold(e.reshape(512, 512) * dp, jnp.sum)

    def C(h, j):
        dp = DP[j]
        dl = drow[h % 2]
        dpb = (dp.reshape(64, 8, 512) - dl[None]).reshape(512, 512).astype(BF)
        eb = E[j]
        ds = eb * dpb
        dv[j] += dot(eb, dos[h % 2])
        dk[j] += dot(ds, qs[h % 2])
        dqT[...] += dot(kT[j], ds)

    def step(t, a1, a2, c):
        if a1:
            for cp in operands(t):
                cp.wait()
        if c:
            dqT[...] = jnp.zeros(dqT.shape, F32)

        def body(j, carry, own=False):
            mx, l, dd = carry
            if a1 and not a2:
                operand(j, own, 0).wait()
            if a1 and a2 and not c:
                operand(j, own, 1).wait()
                kT[j] = kb[j].T
                dk[j] = jnp.zeros(dk.shape[1:], F32)
                dv[j] = jnp.zeros(dv.shape[1:], F32)
            if c:
                C(t - 2, j)
            if a2:
                l_j, d_j = A2(t - 1, j, own)
                l, dd = l + l_j, dd + d_j
            if a1:
                mx = jnp.maximum(mx, A1(t, j, own))
            if c and not a2:
                kg_ref[...] += fold(dk[j] * kb[j].astype(F32), jnp.sum)
                tile_ref[j, :, 0:128] = dk[j].astype(BF)
                tile_ref[j, :, 128:256] = dv[j].astype(BF)
                tile_out(j).start()
            return mx, l, dd
        carry = (jnp.full((8, 512), NEG, F32), jnp.zeros((8, 512), F32), jnp.zeros((8, 512), F32))
        carry = lax.fori_loop(0, J - 1, body, carry, unroll=8)
        mx, l, dd = body(J - 1, carry, True)
        if c:
            h = t - 2
            rl = drow[h % 2 + 2]
            dq = (dqT[...] * (rl[:1] * SC)).T
            x = rows_ref[h, 0].astype(F32)
            rq = lax.rsqrt(jnp.mean(x * x, axis=1, keepdims=True) + EPS)
            dq_raw, gq = norm_back(x, rq, qgain_ref[...], dq)
            dq32[pl.ds(h, 512, stride=8), :] = dq_raw
            gq_ref[...] += fold(gq, jnp.sum)
        if a2:
            h = t - 1
            l1 = jnp.sum(l, axis=0, keepdims=True)
            rl = jnp.broadcast_to(1.0 / l1, (8, 512))
            dl = jnp.sum(dd, axis=0, keepdims=True) * rl[:1]
            drow[h % 2] = jnp.broadcast_to(dl, (8, 512))
            drow[h % 2 + 2] = rl
            rc = rl.T[:, :1]
            dos[h % 2] = (rows_ref[h, 2].astype(F32) * rc).astype(BF)
            qs[h % 2] = (rows_ref[h, 1].astype(F32) * (rc * SC)).astype(BF)
        if a1:
            m = jnp.max(mx, axis=0, keepdims=True)
            mrow[t % 2] = jnp.broadcast_to(m, (8, 512))

    step(0, True, False, False)
    step(1, True, True, False)

    @pl.loop(2, H)
    def _(t):
        step(t, True, True, True)
    step(H, False, True, True)
    step(H + 1, False, False, True)

    dq_ref[...] = dq32[...].astype(BF)
    part_q = jnp.sum(gq_ref[...], axis=0, keepdims=True)
    part_k = jnp.sum(kg_ref[...], axis=0, keepdims=True) / kgain_ref[...]
    row = lax.broadcasted_iota(jnp.int32, (8, 128), 0)
    g_ref[...] = jnp.where(row == 0, part_q, jnp.where(row == 1, part_k, 0.0))
    gcp = pltpu.make_async_copy(g_ref, g_hbm.at[0:8], sem.at[0, J])
    gcp.start()
    gcp.wait()
    for j in range(J + 1):
        tile_out(j).wait()


MESH = pl.DeviceIdType.MESH


def place():
    ctx, y = lax.axis_index("ctx"), lax.axis_index("head")
    return ctx // 8, (ctx // 2) % 4, ctx % 2, y


def peer(z, x, c, y):
    return (z * 8 + x * 2 + c, y)


def hail(devices):
    for d in devices:
        pl.semaphore_signal(pltpu.get_barrier_semaphore(), inc=1, device_id=d, device_id_type=MESH)


def settle(devices):
    pl.semaphore_wait(pltpu.get_barrier_semaphore(), len(devices))


def scatter_kernel(slot_ref, tile_hbm, g_hbm, dk_ref, dv_ref, gout_ref,
                   tile_ref, g_ref, tsem, A, B, cur, R1, R2, T, Q1, Q2, GS, GZ, GX, GY,
                   s0, r0, s1, r1, s2, r2, sg, rg):
    z, x, c, y = place()

    def along(axis, off):
        if axis == "z":
            return peer((z + off) % 4, x, c, y)
        if axis == "x":
            return peer(z, (x + off) % 4, c, y)
        return peer(z, x, c, (y + off) % 4)

    fetch = pltpu.make_async_copy(tile_hbm.at[0:10], tile_ref, tsem.at[0])
    fetch.start()
    gfetch = pltpu.make_async_copy(g_hbm.at[0:8], g_ref, tsem.at[1])
    gfetch.start()
    sib = peer(z, x, 1 - c, y)
    friends = [sib] + [along(a, o) for a in "zxy" for o in (1, 2, 3)]
    hail(friends)
    pending = []

    def send(src, dst, ss, rs, to):
        cp = pltpu.make_async_remote_copy(src_ref=src, dst_ref=dst, send_sem=ss, recv_sem=rs,
                                          device_id=to, device_id_type=MESH)
        cp.start()
        pending.append(cp)
        return cp

    axes = (("z", "x"), ("x", "z"))
    coord = {"z": z, "x": x}

    def block(half, u, w, cc):
        return (u * 8 + w * 2 + cc) if half == 0 else (w * 8 + u * 2 + cc)

    def cols(half):
        return slice(half * 128, half * 128 + 128)

    first = {}

    def fill(half, off):
        u = (coord[axes[half][0]] + off) % 4
        cw = coord[axes[half][1]]

        @pl.loop(0, 4)
        def _(p):
            A[half, off, p] = tile_ref[slot_ref[block(half, u, (cw + p + 2) % 4, 1 - c)], :, cols(half)]

    fetch.wait()
    fill(0, 2)
    fill(1, 2)
    gfetch.wait()
    settle(friends)
    gcp = send(g_ref, GS, sg.at[0], rg.at[0], sib)
    for off in (2, 1, 3, 0):
        for half in (0, 1):
            if off != 2:
                fill(half, off)
            first[half, off] = send(A.at[half, off], B.at[half, off], s0.at[half * 4 + off], r0.at[half * 4 + off], sib)

    def group(G, base, kind):
        me = {"z": z, "x": x, "y": y}[kind]
        cps = [send(G.at[me], G.at[me], sg.at[base + o], rg.at[base + o], along(kind, o)) for o in (1, 2, 3)]
        return cps

    def gsum(G, cps):
        for cp in cps:
            cp.wait_recv()
        return (G[0] + G[1]) + (G[2] + G[3])

    def own_sum(half, off):
        first[half, off].wait_recv()
        u = (coord[axes[half][0]] + off) % 4

        cw = coord[axes[half][1]]

        @pl.loop(0, 4)
        def _(p):
            mine = tile_ref[slot_ref[block(half, u, (cw + p + 2) % 4, c)], :, cols(half)]
            cur[half, off, p] = (mine.astype(F32) + B[half, off, p].astype(F32)).astype(BF)

    def s1send(k, half, src, dst, off):
        return send(src, dst, s1.at[half, k], r1.at[half, k], along(axes[half][0], off))

    c1 = {}
    for half in (0, 1):
        own_sum(half, 2)
        c1[half, 0] = s1send(0, half, cur.at[half, 2, 0:2], R1.at[half, 0], 1)
        c1[half, 1] = s1send(1, half, cur.at[half, 2, 2:4], R1.at[half, 1], 3)
    for half in (0, 1):
        own_sum(half, 1)
        c1[half, 2] = s1send(2, half, cur.at[half, 1, 2:4], R2.at[half, 0, 2:4], 1)
        own_sum(half, 3)
        c1[half, 3] = s1send(3, half, cur.at[half, 3, 0:2], R2.at[half, 1, 0:2], 3)
    gcp.wait_recv()
    GZ[z] = g_ref[...] + GS[...]
    gz = group(GZ, 0, "z")
    for half in (0, 1):
        own_sum(half, 0)
    def merge(half, k, p):
        off = 1 if k == 0 else 3
        cur[half, off, p] = (cur[half, off, p].astype(F32) + R1[half, k, p % 2].astype(F32)).astype(BF)
        c1[half, 4 + p] = s1send(4 + p, half, cur.at[half, off, p], R2.at[half, k, p], off)

    for half in (0, 1):
        c1[half, 0].wait_recv()
        merge(half, 0, 0)
        c1[half, 1].wait_recv()
        merge(half, 1, 3)
    for half in (0, 1):
        merge(half, 0, 1)
        merge(half, 1, 2)
    GX[x] = gsum(GZ, gz)
    gx = group(GX, 3, "x")

    def s2send(k, half, src, dst, off):
        return send(src, dst, s2.at[half, k], r2.at[half, k], along(axes[half][1], off))

    lo, hi = slice(0, 256), slice(256, 512)
    c2 = {}

    def total(half, p):
        c1[half, 4 + p].wait_recv()
        T[half, (p + 2) % 4] = (cur[half, 0, p].astype(F32) + R2[half, 0, p].astype(F32)
                                + R2[half, 1, p].astype(F32)).astype(BF)

    for half in (0, 1):
        c1[half, 2].wait_recv()
        c1[half, 3].wait_recv()
        total(half, 0)
        c2[half, 0] = s2send(0, half, T.at[half, 2, lo], Q1.at[half, 0], 1)
        c2[half, 1] = s2send(1, half, T.at[half, 2, hi], Q1.at[half, 1], 3)
        total(half, 3)
        c2[half, 2] = s2send(2, half, T.at[half, 1, hi], Q2.at[half, 0, hi], 1)
    for half in (0, 1):
        total(half, 1)
        c2[half, 3] = s2send(3, half, T.at[half, 3, lo], Q2.at[half, 1, lo], 3)
        total(half, 2)
    GY[y] = gsum(GX, gx)
    gy = group(GY, 6, "y")
    for half in (0, 1):
        c2[half, 0].wait_recv()
        T[half, 1, lo] = (T[half, 1, lo].astype(F32) + Q1[half, 0].astype(F32)).astype(BF)
        c2[half, 4] = s2send(4, half, T.at[half, 1, lo], Q2.at[half, 0, lo], 1)
        c2[half, 1].wait_recv()
        T[half, 3, hi] = (T[half, 3, hi].astype(F32) + Q1[half, 1].astype(F32)).astype(BF)
        c2[half, 5] = s2send(5, half, T.at[half, 3, hi], Q2.at[half, 1, hi], 3)
    gout_ref[...] = gsum(GY, gy)
    for half in (0, 1):
        for k in (2, 3, 4, 5):
            c2[half, k].wait_recv()
        out = T[half, 0].astype(F32) + Q2[half, 0].astype(F32) + Q2[half, 1].astype(F32)
        if half == 0:
            dk_ref[...] = out
        else:
            dv_ref[...] = out.astype(BF)
    for cp in pending:
        cp.wait_send()


def scatter(slot, tile, g):
    V = functools.partial(pl.BlockSpec, memory_space=pltpu.VMEM)
    D = pltpu.SemaphoreType.DMA
    return pl.pallas_call(
        scatter_kernel,
        out_shape=(jax.ShapeDtypeStruct((512, 128), F32), jax.ShapeDtypeStruct((512, 128), BF),
                   jax.ShapeDtypeStruct((8, 128), F32)),
        in_specs=[pl.BlockSpec(memory_space=pltpu.SMEM), pl.BlockSpec(memory_space=pl.ANY), pl.BlockSpec(memory_space=pl.ANY)],
        out_specs=(V(), V(), V()),
        scratch_shapes=[
            pltpu.VMEM((10, 512, 256), BF), pltpu.VMEM((8, 128), F32), D((2,)),
            pltpu.VMEM((2, 4, 4, 512, 128), BF), pltpu.VMEM((2, 4, 4, 512, 128), BF), pltpu.VMEM((2, 4, 4, 512, 128), BF),
            pltpu.VMEM((2, 2, 2, 512, 128), BF), pltpu.VMEM((2, 2, 4, 512, 128), BF),
            pltpu.VMEM((2, 4, 512, 128), BF), pltpu.VMEM((2, 2, 256, 128), BF), pltpu.VMEM((2, 2, 512, 128), BF),
            pltpu.VMEM((8, 128), F32), pltpu.VMEM((4, 8, 128), F32), pltpu.VMEM((4, 8, 128), F32), pltpu.VMEM((4, 8, 128), F32),
            D((8,)), D((8,)), D((2, 8)), D((2, 8)), D((2, 6)), D((2, 6)), D((10,)), D((10,)),
        ],
        compiler_params=pltpu.CompilerParams(collective_id=1, has_side_effects=True, vmem_limit_bytes=52 * 2 ** 20),
    )(slot, tile, g)


def gather_kernel(k_ref, v_ref, q_hbm, do_hbm, qg_ref, kg_ref, ko_ref, vo_ref, rows_out, cols_out,
                  kn_ref, qb, db, q32, do32, isem, rows, cols, lsem, psem, ss, rs):
    z, x, c, y = place()

    def along(axis, off):
        return peer((z + off) % 4, x, c, y) if axis == "z" else peer(z, (x + off) % 4, c, y)

    sib = peer(z, x, 1 - c, y)
    friends = [sib] + [along(a, o) for a in "zx" for o in (1, 3)]
    hail(friends)
    loads = [pltpu.make_async_copy(q_hbm, qb, isem.at[0]), pltpu.make_async_copy(do_hbm, db, isem.at[1])]
    for cp in loads:
        cp.start()
    _, _, kn = norm_fwd(k_ref[...], kg_ref[...])
    kn_ref[...] = kn
    settle(friends)
    coord = {"z": z, "x": x}
    pending = []
    sibling = []
    count = [0, 0]

    halves = ((kn_ref, ko_ref, "x", "z"), (v_ref, vo_ref, "z", "x"))
    lo, hi, full = slice(0, 256), slice(256, 512), slice(0, 512)

    def block(half, uo, wo, cc=None):
        cc = c if cc is None else cc
        u = (coord[halves[half][2]] + uo) % 4
        w = (coord[halves[half][3]] + wo) % 4
        return u * 2 + w * 8 + cc if half == 0 else u * 8 + w * 2 + cc

    def send(half, uo, wo, rows, to, src=None):
        out = halves[half][1]
        k = count[half]
        count[half] += 1
        b = block(half, uo, wo)
        cp = pltpu.make_async_remote_copy(
            src_ref=out.at[b, rows] if src is None else src, dst_ref=out.at[b, rows],
            send_sem=ss.at[half, k], recv_sem=rs.at[half, k], device_id=to, device_id_type=MESH)
        cp.start()
        pending.append(cp)
        return cp

    local = []
    for half, (src, out, u, w) in enumerate(halves):
        cp = pltpu.make_async_copy(src, out.at[block(half, 0, 0)], lsem.at[half])
        cp.start()
        local.append(cp)
    got = {}
    for half, (src, out, u, w) in enumerate(halves):
        got[half, "u+"] = send(half, 0, 0, full, along(u, 1), src)
        got[half, "u-"] = send(half, 0, 0, full, along(u, 3), src)
    def prep(h):
        x = q32[pl.ds(h, 512, stride=8), :]
        _, _, qn = norm_fwd(x, qg_ref[...])
        d = do32[pl.ds(h, 512, stride=8), :].astype(BF)
        rows[h, 0] = x.astype(BF)
        rows[h, 1] = qn
        rows[h, 2] = d
        cols[h, 0] = qn.T
        cols[h, 1] = d.T
        for n, (src, dst) in enumerate(((rows, rows_out), (cols, cols_out))):
            cp = pltpu.make_async_copy(src.at[h], dst.at[h], psem.at[n, h])
            cp.start()
            local.append(cp)

    for half, (src, out, u, w) in enumerate(halves):
        got[half, 0, "w+"] = send(half, 0, 0, full, along(w, 1), src)
        got[half, 0, "w-"] = send(half, 0, 0, full, along(w, 3), src)
        sibling.append(send(half, 0, 0, full, sib, src))
    for cp in loads:
        cp.wait()
    q32[...] = qb[...].astype(F32)
    do32[...] = db[...].astype(F32)
    prep(0)
    for half, (src, out, u, w) in enumerate(halves):
        got[half, "u+"].wait_recv()
        got[half, "f+"] = send(half, 3, 0, lo, along(u, 1))
        got[half, 3, "w+"] = send(half, 3, 0, full, along(w, 1))
        got[half, 3, "w-"] = send(half, 3, 0, full, along(w, 3))
        sibling.append(send(half, 3, 0, full, sib))
        got[half, "u-"].wait_recv()
        got[half, "f-"] = send(half, 1, 0, hi, along(u, 3))
        got[half, 1, "w+"] = send(half, 1, 0, full, along(w, 1))
        got[half, 1, "w-"] = send(half, 1, 0, full, along(w, 3))
        sibling.append(send(half, 1, 0, full, sib))

    def onward(half, uo):
        w = halves[half][3]
        got[half, uo, "w+"].wait_recv()
        got[half, uo, "g+"] = send(half, uo, 3, lo, along(w, 1))
        sibling.append(send(half, uo, 3, full, sib))
        got[half, uo, "w-"].wait_recv()
        got[half, uo, "g-"] = send(half, uo, 1, hi, along(w, 3))
        sibling.append(send(half, uo, 1, full, sib))

    prep(1)
    for half in (0, 1):
        onward(half, 0)
    prep(2)
    for half, (src, out, u, w) in enumerate(halves):
        got[half, "f+"].wait_recv()
        got[half, "f-"].wait_recv()
        got[half, 2, "w+"] = send(half, 2, 0, full, along(w, 1))
        got[half, 2, "w-"] = send(half, 2, 0, full, along(w, 3))
        sibling.append(send(half, 2, 0, full, sib))
    for uo in (3, 1, 2):
        prep(3 + (uo % 3))
        for half in (0, 1):
            onward(half, uo)
    prep(6)
    prep(7)
    for uo in (0, 3, 1, 2):
        for half in (0, 1):
            got[half, uo, "g+"].wait_recv()
            got[half, uo, "g-"].wait_recv()
            sibling.append(send(half, uo, 2, full, sib))
    for cp in sibling:
        cp.wait_recv()
    for cp in pending:
        cp.wait_send()
    for cp in local:
        cp.wait()


def gather(k, v, q, do, qg, kg):
    D = pltpu.SemaphoreType.DMA
    anys = pl.BlockSpec(memory_space=pl.ANY)
    vm = pl.BlockSpec(memory_space=pltpu.VMEM)
    return pl.pallas_call(
        gather_kernel,
        out_shape=(jax.ShapeDtypeStruct((32, 512, 128), BF), jax.ShapeDtypeStruct((32, 512, 128), BF),
                   jax.ShapeDtypeStruct((8, 3, 512, 128), BF), jax.ShapeDtypeStruct((8, 2, 128, 512), BF)),
        in_specs=[vm, vm, anys, anys, vm, vm],
        out_specs=(anys,) * 4,
        scratch_shapes=[
            pltpu.VMEM((512, 128), BF), pltpu.VMEM((4096, 128), BF), pltpu.VMEM((4096, 128), BF),
            pltpu.VMEM((4096, 128), F32), pltpu.VMEM((4096, 128), F32), D((2,)),
            pltpu.VMEM((8, 3, 512, 128), BF), pltpu.VMEM((8, 2, 128, 512), BF),
            D((2,)), D((2, 8)), D((2, 36)), D((2, 36)),
        ],
        compiler_params=pltpu.CompilerParams(collective_id=0, has_side_effects=True, vmem_limit_bytes=60 * 2 ** 20),
    )(k, v, q, do, qg, kg)


def attn(idx, kn_all, v_all, rows, cols, qg, kg):
    H = rows.shape[0]
    V = functools.partial(pl.BlockSpec, memory_space=pltpu.VMEM)
    A = functools.partial(pl.BlockSpec, memory_space=pl.ANY)
    return pl.pallas_call(
        attn_kernel,
        out_shape=(
            jax.ShapeDtypeStruct((512 * H, 128), BF),
            jax.ShapeDtypeStruct((64, 512, 256), BF),
            jax.ShapeDtypeStruct((32768, 128), F32),
            jax.ShapeDtypeStruct((40,), jnp.int32),
        ),
        in_specs=[pl.BlockSpec(memory_space=pltpu.SMEM), A(), A(), A(), A(), V(), V()],
        out_specs=(V(), A(), A(), pl.BlockSpec(memory_space=pltpu.SMEM)),
        scratch_shapes=[
            pltpu.VMEM((10, 512, 256), BF), pltpu.VMEM((8, 128), F32),
            pltpu.VMEM((H, 3, 512, 128), BF), pltpu.VMEM((H, 2, 128, 512), BF),
            pltpu.VMEM((8, 128), F32), pltpu.VMEM((8, 128), F32),
            pltpu.VMEM((9, 512, 128), BF), pltpu.VMEM((9, 512, 128), BF),
            pltpu.VMEM((9, 128, 512), BF),
            pltpu.VMEM((9, 512, 512), F32), pltpu.VMEM((9, 512, 512), F32), pltpu.VMEM((9, 512, 512), BF),
            pltpu.VMEM((9, 512, 128), F32), pltpu.VMEM((9, 512, 128), F32),
            pltpu.VMEM((128, 512), F32),
            pltpu.VMEM((2, 8, 512), F32), pltpu.VMEM((4, 8, 512), F32),
            pltpu.VMEM((2, 512, 128), BF), pltpu.VMEM((2, 512, 128), BF),
            pltpu.VMEM((512 * H, 128), F32),
            pltpu.SemaphoreType.DMA((3, 10)), pltpu.SemaphoreType.DMA((2, H)),
        ],
        compiler_params=pltpu.CompilerParams(vmem_limit_bytes=60 * 2 ** 20),
    )(idx, kn_all, v_all, rows, cols, qg, kg)


def on_device(q_raw, k_raw, values, dout, q_gain, k_gain, chosen):
    blk, heads, width = q_raw.shape
    k2, v2 = k_raw.reshape(blk, width), values.reshape(blk, width)
    qg, kg = q_gain[None], k_gain[None]
    kn_all, v_all, rows, cols = gather(
        k2, v2, q_raw.reshape(blk * heads, width), dout.reshape(blk * heads, width), qg, kg)
    dq_raw, tile, parts, slot = attn(chosen.reshape(-1), kn_all, v_all, rows, cols, qg, kg)
    dkn, dvalues, sums = scatter(slot, tile, parts)
    xk, rk, _ = norm_fwd(k2, k_gain)
    dk_raw, _ = norm_back(xk, rk, k_gain, dkn)
    return (
        dq_raw.reshape(blk, heads, width),
        dk_raw.astype(BF).reshape(blk, 1, width),
        dvalues.reshape(blk, 1, width),
        sums[0],
        sums[1],
    )


def solution(mesh):
    tok = P("ctx", "head", None)
    return jax.shard_map(
        on_device,
        mesh=mesh,
        in_specs=(tok, tok, tok, tok, P(), P(), tok),
        out_specs=(tok, tok, tok, P(), P()),
        check_vma=False,
    )
```

```python
import functools

import jax, jax.numpy as jnp
from jax import lax
from jax.experimental import pallas as pl
from jax.experimental.pallas import tpu as pltpu
from jax.sharding import PartitionSpec as P

SC = 128 ** -0.5
C2 = SC * 1.4426950408889634
NEG = -1e30
F32 = jnp.float32
BF = jnp.bfloat16

EPS = 1e-06


def norm_fwd(raw, gain):
    x = raw.astype(jnp.float32)
    scale_r = lax.rsqrt(jnp.mean(x * x, axis=-1, keepdims=True) + EPS)
    return (x, scale_r, (x * scale_r * gain).astype(jnp.bfloat16))


def norm_back(x, scale_r, gain, grad_y):
    along = gain * grad_y
    inner = jnp.mean(along * x, axis=-1, keepdims=True)
    grad_x = scale_r * (along - x * scale_r * scale_r * inner)
    return (grad_x, grad_y * x * scale_r)


def dot(a, b):
    return lax.dot_general(a, b, (((1,), (0,)), ((), ())), preferred_element_type=F32)

def fold(x, op):
    return op(x.reshape(x.shape[0] // 8, 8, x.shape[1]), axis=0)

def attn_kernel(idx_ref, kn_hbm, v_hbm, rows_hbm, cols_hbm, qgain_ref, kgain_ref,
                dq_hbm, tile_hbm, g_hbm, slot_ref, dq_ref, tile_ref, g_ref, rows_ref, cols_ref, kg_ref, gq_ref,
                kb, vb, kT, S, DP, E, dk, dv, dqT, mrow, drow, qs, dos, dq32, sem, hsem):
    H = rows_hbm.shape[0]
    J = 9
    me = lax.axis_index("ctx")
    def operand(j, own, n):
        blk = me if own else jnp.maximum(idx_ref[j], 0)
        src, dst = ((kn_hbm, kb), (v_hbm, vb))[n]
        return pltpu.make_async_copy(src.at[blk], dst.at[j], sem.at[n, j])

    def tile_out(j):
        return pltpu.make_async_copy(tile_ref.at[j], tile_hbm.at[j], sem.at[2, j])

    def operands(h):
        return (pltpu.make_async_copy(rows_hbm.at[h], rows_ref.at[h], hsem.at[0, h]),
                pltpu.make_async_copy(cols_hbm.at[h], cols_ref.at[h], hsem.at[1, h]))

    for cp in operands(0):
        cp.start()
    for n in (0, 1):
        for j in range(J):
            operand(j, j == J - 1, n).start()
    for h in range(1, H):
        for cp in operands(h):
            cp.start()
    for b in range(40):
        slot_ref[b] = J
    for j in range(J - 1):
        slot_ref[jnp.where(idx_ref[j] >= 0, idx_ref[j], 32)] = j
    slot_ref[me] = J - 1
    kg_ref[...] = jnp.zeros(kg_ref.shape, F32)
    gq_ref[...] = jnp.zeros(gq_ref.shape, F32)
    tile_ref[J] = jnp.zeros(tile_ref.shape[1:], BF)
    tile_out(J).start()

    rows = lax.broadcasted_iota(jnp.int32, (512, 512), 0)
    cols = lax.broadcasted_iota(jnp.int32, (512, 512), 1)

    def A1(h, j, own):
        s = dot(kb[j], cols_ref[h, 0])
        if own:
            s = jnp.where(rows <= cols, s, NEG)
        S[j] = s
        cm = fold(s, jnp.max)
        if not own:
            cm = jnp.where(idx_ref[j] >= 0, cm, NEG)
        return cm

    def A2(h, j, own):
        m = mrow[h % 2]
        if not own:
            m = jnp.where(idx_ref[j] >= 0, m, 1e30)
        s = S[j]
        e = jnp.exp2((s.reshape(64, 8, 512) - m[None]) * C2)
        l = jnp.sum(e, axis=0)
        eb = e.reshape(512, 512).astype(BF)
        E[j] = eb
        dp = dot(vb[j], cols_ref[h, 1])
        DP[j] = dp
        return l, fold(e.reshape(512, 512) * dp, jnp.sum)

    def C(h, j):
        dp = DP[j]
        dl = drow[h % 2]
        dpb = (dp.reshape(64, 8, 512) - dl[None]).reshape(512, 512).astype(BF)
        eb = E[j]
        ds = eb * dpb
        dv[j] += dot(eb, dos[h % 2])
        dk[j] += dot(ds, qs[h % 2])
        dqT[...] += dot(kT[j], ds)

    def step(t, a1, a2, c):
        if a1:
            for cp in operands(t):
                cp.wait()
        if c:
            dqT[...] = jnp.zeros(dqT.shape, F32)

        def body(j, carry, own=False):
            mx, l, dd = carry
            if a1 and not a2:
                operand(j, own, 0).wait()
            if a1 and a2 and not c:
                operand(j, own, 1).wait()
                kT[j] = kb[j].T
                dk[j] = jnp.zeros(dk.shape[1:], F32)
                dv[j] = jnp.zeros(dv.shape[1:], F32)
            if c:
                C(t - 2, j)
            if a2:
                l_j, d_j = A2(t - 1, j, own)
                l, dd = l + l_j, dd + d_j
            if a1:
                mx = jnp.maximum(mx, A1(t, j, own))
            if c and not a2:
                kg_ref[...] += fold(dk[j] * kb[j].astype(F32), jnp.sum)
                tile_ref[j, :, 0:128] = dk[j].astype(BF)
                tile_ref[j, :, 128:256] = dv[j].astype(BF)
                tile_out(j).start()
            return mx, l, dd
        carry = (jnp.full((8, 512), NEG, F32), jnp.zeros((8, 512), F32), jnp.zeros((8, 512), F32))
        carry = lax.fori_loop(0, J - 1, body, carry, unroll=8)
        mx, l, dd = body(J - 1, carry, True)
        if c:
            h = t - 2
            rl = drow[h % 2 + 2]
            dq = (dqT[...] * (rl[:1] * SC)).T
            x = rows_ref[h, 0].astype(F32)
            rq = lax.rsqrt(jnp.mean(x * x, axis=1, keepdims=True) + EPS)
            dq_raw, gq = norm_back(x, rq, qgain_ref[...], dq)
            dq32[pl.ds(h, 512, stride=8), :] = dq_raw
            gq_ref[...] += fold(gq, jnp.sum)
        if a2:
            h = t - 1
            l1 = jnp.sum(l, axis=0, keepdims=True)
            rl = jnp.broadcast_to(1.0 / l1, (8, 512))
            dl = jnp.sum(dd, axis=0, keepdims=True) * rl[:1]
            drow[h % 2] = jnp.broadcast_to(dl, (8, 512))
            drow[h % 2 + 2] = rl
            rc = rl.T[:, :1]
            dos[h % 2] = (rows_ref[h, 2].astype(F32) * rc).astype(BF)
            qs[h % 2] = (rows_ref[h, 1].astype(F32) * (rc * SC)).astype(BF)
        if a1:
            m = jnp.max(mx, axis=0, keepdims=True)
            mrow[t % 2] = jnp.broadcast_to(m, (8, 512))

    step(0, True, False, False)
    step(1, True, True, False)

    @pl.loop(2, H)
    def _(t):
        step(t, True, True, True)
    step(H, False, True, True)
    step(H + 1, False, False, True)

    part_q = jnp.sum(gq_ref[...], axis=0, keepdims=True)
    part_k = jnp.sum(kg_ref[...], axis=0, keepdims=True) / kgain_ref[...]
    row = lax.broadcasted_iota(jnp.int32, (8, 128), 0)
    g_ref[...] = jnp.where(row == 0, part_q, jnp.where(row == 1, part_k, 0.0))
    gcp = pltpu.make_async_copy(g_ref, g_hbm.at[0:8], sem.at[0, J])
    gcp.start()

    def dq_out(b):
        rows = pl.ds(b * 1024, 1024)
        return pltpu.make_async_copy(dq_ref.at[rows], dq_hbm.at[rows], hsem.at[0, b])

    for b in range(4):
        rows = pl.ds(b * 1024, 1024)
        dq_ref[rows] = dq32[rows].astype(BF)
        dq_out(b).start()
    gcp.wait()
    for j in range(J + 1):
        tile_out(j).wait()
    for b in range(4):
        dq_out(b).wait()


MESH = pl.DeviceIdType.MESH


def place():
    ctx, y = lax.axis_index("ctx"), lax.axis_index("head")
    return ctx // 8, (ctx // 2) % 4, ctx % 2, y


def peer(z, x, c, y):
    return (z * 8 + x * 2 + c, y)


def hail(devices):
    for d in devices:
        pl.semaphore_signal(pltpu.get_barrier_semaphore(), inc=1, device_id=d, device_id_type=MESH)


def settle(devices):
    pl.semaphore_wait(pltpu.get_barrier_semaphore(), len(devices))


def scatter_kernel(slot_ref, tile_hbm, g_hbm, dk_ref, dv_ref, gout_ref,
                   tile_ref, g_ref, tsem, A, B, cur, R1, R2, T, Q1, Q2, GS, GZ, GX, GY,
                   s0, r0, s1, r1, s2, r2, sg, rg):
    z, x, c, y = place()

    def along(axis, off):
        if axis == "z":
            return peer((z + off) % 4, x, c, y)
        if axis == "x":
            return peer(z, (x + off) % 4, c, y)
        return peer(z, x, c, (y + off) % 4)

    fetch = pltpu.make_async_copy(tile_hbm.at[0:10], tile_ref, tsem.at[0])
    fetch.start()
    gfetch = pltpu.make_async_copy(g_hbm.at[0:8], g_ref, tsem.at[1])
    gfetch.start()
    sib = peer(z, x, 1 - c, y)
    friends = [sib] + [along(a, o) for a in "zxy" for o in (1, 2, 3)]
    hail(friends)
    pending = []

    def send(src, dst, ss, rs, to):
        cp = pltpu.make_async_remote_copy(src_ref=src, dst_ref=dst, send_sem=ss, recv_sem=rs,
                                          device_id=to, device_id_type=MESH)
        cp.start()
        pending.append(cp)
        return cp

    axes = (("z", "x"), ("x", "z"))
    coord = {"z": z, "x": x}

    def block(half, u, w, cc):
        return (u * 8 + w * 2 + cc) if half == 0 else (w * 8 + u * 2 + cc)

    def cols(half):
        return slice(half * 128, half * 128 + 128)

    first = {}

    def fill(half, off):
        u = (coord[axes[half][0]] + off) % 4
        cw = coord[axes[half][1]]

        @pl.loop(0, 4)
        def _(p):
            A[half, off, p] = tile_ref[slot_ref[block(half, u, (cw + p + 2) % 4, 1 - c)], :, cols(half)]

    fetch.wait()
    fill(0, 2)
    fill(1, 2)
    gfetch.wait()
    settle(friends)
    gcp = send(g_ref, GS, sg.at[0], rg.at[0], sib)
    for off in (2, 1, 3, 0):
        for half in (0, 1):
            if off != 2:
                fill(half, off)
            first[half, off] = send(A.at[half, off], B.at[half, off], s0.at[half * 4 + off], r0.at[half * 4 + off], sib)

    def group(G, base, kind):
        me = {"z": z, "x": x, "y": y}[kind]
        cps = [send(G.at[me], G.at[me], sg.at[base + o], rg.at[base + o], along(kind, o)) for o in (1, 2, 3)]
        return cps

    def gsum(G, cps):
        for cp in cps:
            cp.wait_recv()
        return (G[0] + G[1]) + (G[2] + G[3])

    def own_sum(half, off):
        first[half, off].wait_recv()
        u = (coord[axes[half][0]] + off) % 4

        cw = coord[axes[half][1]]

        @pl.loop(0, 4)
        def _(p):
            mine = tile_ref[slot_ref[block(half, u, (cw + p + 2) % 4, c)], :, cols(half)]
            cur[half, off, p] = (mine.astype(F32) + B[half, off, p].astype(F32)).astype(BF)

    def s1send(k, half, src, dst, off):
        return send(src, dst, s1.at[half, k], r1.at[half, k], along(axes[half][0], off))

    c1 = {}
    for half in (0, 1):
        own_sum(half, 2)
        c1[half, 0] = s1send(0, half, cur.at[half, 2, 0:2], R1.at[half, 0], 1)
        c1[half, 1] = s1send(1, half, cur.at[half, 2, 2:4], R1.at[half, 1], 3)
    for half in (0, 1):
        own_sum(half, 1)
        c1[half, 2] = s1send(2, half, cur.at[half, 1, 2:4], R2.at[half, 0, 2:4], 1)
        own_sum(half, 3)
        c1[half, 3] = s1send(3, half, cur.at[half, 3, 0:2], R2.at[half, 1, 0:2], 3)
    gcp.wait_recv()
    GZ[z] = g_ref[...] + GS[...]
    gz = group(GZ, 0, "z")
    for half in (0, 1):
        own_sum(half, 0)
    def merge(half, k, p):
        off = 1 if k == 0 else 3
        cur[half, off, p] = (cur[half, off, p].astype(F32) + R1[half, k, p % 2].astype(F32)).astype(BF)
        c1[half, 4 + p] = s1send(4 + p, half, cur.at[half, off, p], R2.at[half, k, p], off)

    for half in (0, 1):
        c1[half, 0].wait_recv()
        merge(half, 0, 0)
        c1[half, 1].wait_recv()
        merge(half, 1, 3)
    for half in (0, 1):
        merge(half, 0, 1)
        merge(half, 1, 2)
    GX[x] = gsum(GZ, gz)
    gx = group(GX, 3, "x")

    def s2send(k, half, src, dst, off):
        return send(src, dst, s2.at[half, k], r2.at[half, k], along(axes[half][1], off))

    lo, hi = slice(0, 256), slice(256, 512)
    c2 = {}

    def total(half, p):
        c1[half, 4 + p].wait_recv()
        T[half, (p + 2) % 4] = (cur[half, 0, p].astype(F32) + R2[half, 0, p].astype(F32)
                                + R2[half, 1, p].astype(F32)).astype(BF)

    for half in (0, 1):
        c1[half, 2].wait_recv()
        c1[half, 3].wait_recv()
        total(half, 0)
        c2[half, 0] = s2send(0, half, T.at[half, 2, lo], Q1.at[half, 0], 1)
        c2[half, 1] = s2send(1, half, T.at[half, 2, hi], Q1.at[half, 1], 3)
        total(half, 3)
        c2[half, 2] = s2send(2, half, T.at[half, 1, hi], Q2.at[half, 0, hi], 1)
    for half in (0, 1):
        total(half, 1)
        c2[half, 3] = s2send(3, half, T.at[half, 3, lo], Q2.at[half, 1, lo], 3)
        total(half, 2)
    GY[y] = gsum(GX, gx)
    gy = group(GY, 6, "y")
    for half in (0, 1):
        c2[half, 0].wait_recv()
        T[half, 1, lo] = (T[half, 1, lo].astype(F32) + Q1[half, 0].astype(F32)).astype(BF)
        c2[half, 4] = s2send(4, half, T.at[half, 1, lo], Q2.at[half, 0, lo], 1)
        c2[half, 1].wait_recv()
        T[half, 3, hi] = (T[half, 3, hi].astype(F32) + Q1[half, 1].astype(F32)).astype(BF)
        c2[half, 5] = s2send(5, half, T.at[half, 3, hi], Q2.at[half, 1, hi], 3)
    gout_ref[...] = gsum(GY, gy)
    for half in (0, 1):
        for k in (2, 3, 4, 5):
            c2[half, k].wait_recv()
        out = T[half, 0].astype(F32) + Q2[half, 0].astype(F32) + Q2[half, 1].astype(F32)
        if half == 0:
            dk_ref[...] = out
        else:
            dv_ref[...] = out.astype(BF)
    for cp in pending:
        cp.wait_send()


def scatter(slot, tile, g):
    V = functools.partial(pl.BlockSpec, memory_space=pltpu.VMEM)
    D = pltpu.SemaphoreType.DMA
    return pl.pallas_call(
        scatter_kernel,
        out_shape=(jax.ShapeDtypeStruct((512, 128), F32), jax.ShapeDtypeStruct((512, 128), BF),
                   jax.ShapeDtypeStruct((8, 128), F32)),
        in_specs=[pl.BlockSpec(memory_space=pltpu.SMEM), pl.BlockSpec(memory_space=pl.ANY), pl.BlockSpec(memory_space=pl.ANY)],
        out_specs=(V(), V(), V()),
        scratch_shapes=[
            pltpu.VMEM((10, 512, 256), BF), pltpu.VMEM((8, 128), F32), D((2,)),
            pltpu.VMEM((2, 4, 4, 512, 128), BF), pltpu.VMEM((2, 4, 4, 512, 128), BF), pltpu.VMEM((2, 4, 4, 512, 128), BF),
            pltpu.VMEM((2, 2, 2, 512, 128), BF), pltpu.VMEM((2, 2, 4, 512, 128), BF),
            pltpu.VMEM((2, 4, 512, 128), BF), pltpu.VMEM((2, 2, 256, 128), BF), pltpu.VMEM((2, 2, 512, 128), BF),
            pltpu.VMEM((8, 128), F32), pltpu.VMEM((4, 8, 128), F32), pltpu.VMEM((4, 8, 128), F32), pltpu.VMEM((4, 8, 128), F32),
            D((8,)), D((8,)), D((2, 8)), D((2, 8)), D((2, 6)), D((2, 6)), D((10,)), D((10,)),
        ],
        compiler_params=pltpu.CompilerParams(collective_id=1, has_side_effects=True, vmem_limit_bytes=52 * 2 ** 20),
    )(slot, tile, g)


def gather_kernel(k_ref, v_ref, q_hbm, do_hbm, qg_ref, kg_ref, ko_ref, vo_ref, rows_out, cols_out,
                  kn_ref, qb, db, q32, do32, isem, rows, cols, lsem, psem, ss, rs):
    z, x, c, y = place()

    def along(axis, off):
        return peer((z + off) % 4, x, c, y) if axis == "z" else peer(z, (x + off) % 4, c, y)

    sib = peer(z, x, 1 - c, y)
    friends = [sib] + [along(a, o) for a in "zx" for o in (1, 3)]
    hail(friends)
    loads = [pltpu.make_async_copy(q_hbm, qb, isem.at[0]), pltpu.make_async_copy(do_hbm, db, isem.at[1])]
    for cp in loads:
        cp.start()
    _, _, kn = norm_fwd(k_ref[...], kg_ref[...])
    kn_ref[...] = kn
    settle(friends)
    coord = {"z": z, "x": x}
    pending = []
    sibling = []
    count = [0, 0]

    halves = ((kn_ref, ko_ref, "x", "z"), (v_ref, vo_ref, "z", "x"))
    lo, hi, full = slice(0, 256), slice(256, 512), slice(0, 512)

    def block(half, uo, wo, cc=None):
        cc = c if cc is None else cc
        u = (coord[halves[half][2]] + uo) % 4
        w = (coord[halves[half][3]] + wo) % 4
        return u * 2 + w * 8 + cc if half == 0 else u * 8 + w * 2 + cc

    def send(half, uo, wo, rows, to, src=None):
        out = halves[half][1]
        k = count[half]
        count[half] += 1
        b = block(half, uo, wo)
        cp = pltpu.make_async_remote_copy(
            src_ref=out.at[b, rows] if src is None else src, dst_ref=out.at[b, rows],
            send_sem=ss.at[half, k], recv_sem=rs.at[half, k], device_id=to, device_id_type=MESH)
        cp.start()
        pending.append(cp)
        return cp

    local = []
    for half, (src, out, u, w) in enumerate(halves):
        cp = pltpu.make_async_copy(src, out.at[block(half, 0, 0)], lsem.at[half])
        cp.start()
        local.append(cp)
    got = {}
    for half, (src, out, u, w) in enumerate(halves):
        got[half, "u+"] = send(half, 0, 0, full, along(u, 1), src)
        got[half, "u-"] = send(half, 0, 0, full, along(u, 3), src)
    def prep(h):
        x = q32[pl.ds(h, 512, stride=8), :]
        _, _, qn = norm_fwd(x, qg_ref[...])
        d = do32[pl.ds(h, 512, stride=8), :].astype(BF)
        rows[h, 0] = x.astype(BF)
        rows[h, 1] = qn
        rows[h, 2] = d
        cols[h, 0] = qn.T
        cols[h, 1] = d.T
        for n, (src, dst) in enumerate(((rows, rows_out), (cols, cols_out))):
            cp = pltpu.make_async_copy(src.at[h], dst.at[h], psem.at[n, h])
            cp.start()
            local.append(cp)

    for half, (src, out, u, w) in enumerate(halves):
        got[half, 0, "w+"] = send(half, 0, 0, full, along(w, 1), src)
        got[half, 0, "w-"] = send(half, 0, 0, full, along(w, 3), src)
        sibling.append(send(half, 0, 0, full, sib, src))
    for cp in loads:
        cp.wait()
    q32[...] = qb[...].astype(F32)
    do32[...] = db[...].astype(F32)
    prep(0)
    for half, (src, out, u, w) in enumerate(halves):
        got[half, "u+"].wait_recv()
        got[half, "f+"] = send(half, 3, 0, lo, along(u, 1))
        got[half, 3, "w+"] = send(half, 3, 0, full, along(w, 1))
        got[half, 3, "w-"] = send(half, 3, 0, full, along(w, 3))
        sibling.append(send(half, 3, 0, full, sib))
        got[half, "u-"].wait_recv()
        got[half, "f-"] = send(half, 1, 0, hi, along(u, 3))
        got[half, 1, "w+"] = send(half, 1, 0, full, along(w, 1))
        got[half, 1, "w-"] = send(half, 1, 0, full, along(w, 3))
        sibling.append(send(half, 1, 0, full, sib))

    def onward(half, uo):
        w = halves[half][3]
        got[half, uo, "w+"].wait_recv()
        got[half, uo, "g+"] = send(half, uo, 3, lo, along(w, 1))
        sibling.append(send(half, uo, 3, full, sib))
        got[half, uo, "w-"].wait_recv()
        got[half, uo, "g-"] = send(half, uo, 1, hi, along(w, 3))
        sibling.append(send(half, uo, 1, full, sib))

    prep(1)
    for half in (0, 1):
        onward(half, 0)
    prep(2)
    for half, (src, out, u, w) in enumerate(halves):
        got[half, "f+"].wait_recv()
        got[half, "f-"].wait_recv()
        got[half, 2, "w+"] = send(half, 2, 0, full, along(w, 1))
        got[half, 2, "w-"] = send(half, 2, 0, full, along(w, 3))
        sibling.append(send(half, 2, 0, full, sib))
    for uo in (3, 1, 2):
        prep(3 + (uo % 3))
        for half in (0, 1):
            onward(half, uo)
    prep(6)
    prep(7)
    for uo in (0, 3, 1, 2):
        for half in (0, 1):
            got[half, uo, "g+"].wait_recv()
            got[half, uo, "g-"].wait_recv()
            sibling.append(send(half, uo, 2, full, sib))
    for cp in sibling:
        cp.wait_recv()
    for cp in pending:
        cp.wait_send()
    for cp in local:
        cp.wait()


def gather(k, v, q, do, qg, kg):
    D = pltpu.SemaphoreType.DMA
    anys = pl.BlockSpec(memory_space=pl.ANY)
    vm = pl.BlockSpec(memory_space=pltpu.VMEM)
    return pl.pallas_call(
        gather_kernel,
        out_shape=(jax.ShapeDtypeStruct((32, 512, 128), BF), jax.ShapeDtypeStruct((32, 512, 128), BF),
                   jax.ShapeDtypeStruct((8, 3, 512, 128), BF), jax.ShapeDtypeStruct((8, 2, 128, 512), BF)),
        in_specs=[vm, vm, anys, anys, vm, vm],
        out_specs=(anys,) * 4,
        scratch_shapes=[
            pltpu.VMEM((512, 128), BF), pltpu.VMEM((4096, 128), BF), pltpu.VMEM((4096, 128), BF),
            pltpu.VMEM((4096, 128), F32), pltpu.VMEM((4096, 128), F32), D((2,)),
            pltpu.VMEM((8, 3, 512, 128), BF), pltpu.VMEM((8, 2, 128, 512), BF),
            D((2,)), D((2, 8)), D((2, 36)), D((2, 36)),
        ],
        compiler_params=pltpu.CompilerParams(collective_id=0, has_side_effects=True, vmem_limit_bytes=60 * 2 ** 20),
    )(k, v, q, do, qg, kg)


def attn(idx, kn_all, v_all, rows, cols, qg, kg):
    H = rows.shape[0]
    V = functools.partial(pl.BlockSpec, memory_space=pltpu.VMEM)
    A = functools.partial(pl.BlockSpec, memory_space=pl.ANY)
    return pl.pallas_call(
        attn_kernel,
        out_shape=(
            jax.ShapeDtypeStruct((512 * H, 128), BF),
            jax.ShapeDtypeStruct((64, 512, 256), BF),
            jax.ShapeDtypeStruct((32768, 128), F32),
            jax.ShapeDtypeStruct((40,), jnp.int32),
        ),
        in_specs=[pl.BlockSpec(memory_space=pltpu.SMEM), A(), A(), A(), A(), V(), V()],
        out_specs=(A(), A(), A(), pl.BlockSpec(memory_space=pltpu.SMEM)),
        scratch_shapes=[
            pltpu.VMEM((512 * H, 128), BF), pltpu.VMEM((10, 512, 256), BF), pltpu.VMEM((8, 128), F32),
            pltpu.VMEM((H, 3, 512, 128), BF), pltpu.VMEM((H, 2, 128, 512), BF),
            pltpu.VMEM((8, 128), F32), pltpu.VMEM((8, 128), F32),
            pltpu.VMEM((9, 512, 128), BF), pltpu.VMEM((9, 512, 128), BF),
            pltpu.VMEM((9, 128, 512), BF),
            pltpu.VMEM((9, 512, 512), F32), pltpu.VMEM((9, 512, 512), F32), pltpu.VMEM((9, 512, 512), BF),
            pltpu.VMEM((9, 512, 128), F32), pltpu.VMEM((9, 512, 128), F32),
            pltpu.VMEM((128, 512), F32),
            pltpu.VMEM((2, 8, 512), F32), pltpu.VMEM((4, 8, 512), F32),
            pltpu.VMEM((2, 512, 128), BF), pltpu.VMEM((2, 512, 128), BF),
            pltpu.VMEM((512 * H, 128), F32),
            pltpu.SemaphoreType.DMA((3, 10)), pltpu.SemaphoreType.DMA((2, H)),
        ],
        compiler_params=pltpu.CompilerParams(vmem_limit_bytes=60 * 2 ** 20),
    )(idx, kn_all, v_all, rows, cols, qg, kg)


def on_device(q_raw, k_raw, values, dout, q_gain, k_gain, chosen):
    blk, heads, width = q_raw.shape
    k2, v2 = k_raw.reshape(blk, width), values.reshape(blk, width)
    qg, kg = q_gain[None], k_gain[None]
    kn_all, v_all, rows, cols = gather(
        k2, v2, q_raw.reshape(blk * heads, width), dout.reshape(blk * heads, width), qg, kg)
    dq_raw, tile, parts, slot = attn(chosen.reshape(-1), kn_all, v_all, rows, cols, qg, kg)
    dkn, dvalues, sums = scatter(slot, tile, parts)
    xk, rk, _ = norm_fwd(k2, k_gain)
    dk_raw, _ = norm_back(xk, rk, k_gain, dkn)
    return (
        dq_raw.reshape(blk, heads, width),
        dk_raw.astype(BF).reshape(blk, 1, width),
        dvalues.reshape(blk, 1, width),
        sums[0],
        sums[1],
    )


def solution(mesh):
    tok = P("ctx", "head", None)
    return jax.shard_map(
        on_device,
        mesh=mesh,
        in_specs=(tok, tok, tok, tok, P(), P(), tok),
        out_specs=(tok, tok, tok, P(), P()),
        check_vma=False,
    )
```
